32 devices in a mesh: ctx: 4 (over y, x), fsdp: 8 (over z, core).
Axes of the slice: x: 2, y: 2, z: 4, core: 2. Of those that a mesh axis runs over, the one named last changes fastest.
Arguments:
- tokens: bfloat16 [8, 768, 2048], P('fsdp', 'ctx'), may hold values from -16 to 16
- cotangent: bfloat16 [8, 768, 2048], P('fsdp', 'ctx'), may hold values from -6 to 6
- norm_attn: bfloat16 [2048], P('fsdp'), may hold values from 0.25 to 1.75
- w_qkv: bfloat16 [2048, 4096], P('fsdp'), may hold values from -0.1875 to 0.1875
- w_out: bfloat16 [2048, 2048], P('fsdp'), may hold values from -0.5 to 0.5
- norm_ffn: bfloat16 [2048], P('fsdp'), may hold values from 0.25 to 1.75
- w_gate: bfloat16 [8192, 2048], P('fsdp'), may hold values from -0.125 to 0.125
- w_up: bfloat16 [8192, 2048], P('fsdp'), may hold values from -0.125 to 0.125
- w_down: bfloat16 [8192, 2048], P('fsdp'), may hold values from -0.0625 to 0.0625
- seq_len: int32 [8], P('fsdp'), may hold values from 577 to 768, as said below
- window: int32 [8], P('fsdp'), may hold values from 256 to 512, as said below
- global_pos: int32 [8, 64], P('fsdp'), may hold values from 0 to 576, as said below
Outputs:
- layer_out: bfloat16 [8, 768, 2048], P('fsdp', 'ctx')
- d_tokens: float32 [8, 768, 2048], P('fsdp', 'ctx')
- d_norm_attn: float32 [2048], P('fsdp')
- d_w_qkv: float32 [2048, 4096], P('fsdp')
- d_w_out: float32 [2048, 2048], P('fsdp')
- d_norm_ffn: float32 [2048], P('fsdp')
- d_w_gate: float32 [8192, 2048], P('fsdp')
- d_w_up: float32 [8192, 2048], P('fsdp')
- d_w_down: float32 [8192, 2048], P('fsdp')
The draws below stay inside these ranges and needn't reach their ends.
Inputs may be any that keep to these rules, and one draw needn't show every extreme that they name: `seq_len`: one entry is 768 and another 768 - 191. `window`: one entry is 512 and another half of 512, rounded down. `global_pos`: each row rises strictly, starts with 0 and ends with 576.
All inputs are finite; a program needn't handle non-finite values.
Results may differ from the reference program's by a relative error of at most 0.022.
Values may be sent and summed in bfloat16 or wider, within the bound.
No kernel may reach another device: no remote copies, remote signals or barrier semaphores. Data moves between devices by JAX's collectives and lax.ppermute only.
A program may use at most 832 MiB of HBM per device.

```python
import jax
import jax.numpy as jnp
from jax import lax

D = 2048
QUERY_HEADS = 16
KEY_VALUE_HEADS = 8
HEAD_WIDTH = 128
FF = 8192
WINDOW = 512
G = 64
TOK_DEV = 192
SEQS = 8
SEQUENCE_LENGTH = 768
QKV = 4096


def draw_tokens(key, part):
    key = jax.random.fold_in(key, 11)
    row_key, column_key, entry_key = jax.random.split(key, 3)
    row_scale = jnp.exp(jax.random.uniform(row_key, (SEQS, SEQUENCE_LENGTH, 1), jnp.float32, -1.15, 1.15))
    column_scale = jnp.exp(jax.random.uniform(column_key, (1, 1, D), jnp.float32, -1.15, 1.15))
    values = jax.random.normal(entry_key, (SEQS, SEQUENCE_LENGTH, D), jnp.float32) * row_scale * column_scale
    return jnp.clip(values, -16.0, 16.0).astype(jnp.bfloat16)


def draw_seq_len(key, part):
    key = jax.random.fold_in(key, 5)
    value_key, pick_key = jax.random.split(key)
    lengths = jax.random.randint(value_key, (SEQS,), SEQUENCE_LENGTH - TOK_DEV + 1, SEQUENCE_LENGTH + 1)
    shuffled = jax.random.permutation(pick_key, SEQS)
    lengths = lengths.at[shuffled[0]].set(SEQUENCE_LENGTH)
    return lengths.at[shuffled[1]].set(SEQUENCE_LENGTH - TOK_DEV + 1).astype(jnp.int32)


def draw_window(key, part):
    key = jax.random.fold_in(key, 7)
    value_key, pick_key = jax.random.split(key)
    widths = jax.random.randint(value_key, (SEQS,), WINDOW // 2, WINDOW + 1)
    shuffled = jax.random.permutation(pick_key, SEQS)
    widths = widths.at[shuffled[0]].set(WINDOW)
    return widths.at[shuffled[1]].set(WINDOW // 2).astype(jnp.int32)


def draw_global_pos(key, part):
    key = jax.random.fold_in(key, 17)
    row_keys = jax.random.split(key, SEQS)

    def one_row(row_key):
        shuffled = jax.random.permutation(row_key, SEQUENCE_LENGTH - TOK_DEV - 1) + 1
        chosen = jnp.sort(shuffled[:G - 2]).astype(jnp.int32)
        return jnp.concatenate([jnp.zeros((1,), jnp.int32), chosen, jnp.full((1,), SEQUENCE_LENGTH - TOK_DEV, jnp.int32)])
    return jax.vmap(one_row)(row_keys)


def level_of(stream_key, shape, cuts, least, largest):
    loudness = 1.0
    for axis_at, shards_of in cuts:
        draws = jax.random.uniform(jax.random.fold_in(jax.random.fold_in(stream_key, 6), axis_at), (shards_of,), jnp.float32, least / len(cuts), largest / len(cuts))
        loudness = loudness * jnp.repeat(jnp.exp(draws), shape[axis_at] // shards_of).reshape((-1,) + (1,) * (len(shape) - 1 - axis_at))
    return loudness


def scatter_about(key, extent, width, bound, cuts=(), kind=jnp.bfloat16):
    result = width * jax.random.normal(key, extent, jnp.float32)
    if cuts:
        result = result * level_of(key, extent, cuts, -0.22, 0.18)
    return jnp.clip(result, -bound, bound).astype(kind)


def setup_inputs(seed: int = 0) -> dict:
    streams_of = jax.random.split(jax.random.key(seed), 13)
    return {
        "tokens": draw_tokens(jax.random.fold_in(streams_of[12], 71), 0),
        "cotangent": scatter_about(streams_of[1], (SEQS, SEQUENCE_LENGTH, D), 1.0, 6.0, ((0, 8), (1, 4))),
        "norm_attn": jnp.clip(1.0 + 0.15 * jax.random.normal(streams_of[2], (D,), jnp.float32), 0.25, 1.75).astype(jnp.bfloat16),
        "w_qkv": scatter_about(streams_of[3], (D, QKV), (D // 2) ** -0.5, 0.1875, ((0, 8),)),
        "w_out": scatter_about(streams_of[4], (QUERY_HEADS * HEAD_WIDTH, D), (QUERY_HEADS * HEAD_WIDTH // 16) ** -0.5, 0.5, ((0, 8),)),
        "norm_ffn": jnp.clip(1.0 + 0.15 * jax.random.normal(streams_of[5], (D,), jnp.float32), 0.25, 1.75).astype(jnp.bfloat16),
        "w_gate": scatter_about(streams_of[6], (FF, D), D ** -0.5, 0.125, ((0, 8),)),
        "w_up": scatter_about(streams_of[7], (FF, D), D ** -0.5, 0.125, ((0, 8),)),
        "w_down": scatter_about(streams_of[8], (FF, D), FF ** -0.5, 0.0625, ((0, 8),)),
        "seq_len": draw_seq_len(jax.random.fold_in(streams_of[12], 71), 0),
        "window": draw_window(jax.random.fold_in(streams_of[12], 71), 0),
        "global_pos": draw_global_pos(jax.random.fold_in(streams_of[12], 71), 0),
    }


NORM_EPS = 1e-05
NEGATIVE_FILLER = -1e+30
ROPE_BASE = 1000000.0
PRECISE_DOT = lax.Precision.HIGHEST

@jax.custom_vjp
def lowered_input(v):
    return lax.optimization_barrier(v.astype(jnp.bfloat16)).astype(jnp.float32)

@jax.custom_vjp
def low_back(v):
    return v

def low_keep(v):
    return (lowered_input(v), None)

def low_pass(kept, grad):
    return (grad,)

def back_keep(v):
    return (v, None)

def back_low(kept, grad):
    return (lowered_input(grad),)
lowered_input.defvjp(low_keep, low_pass)
low_back.defvjp(back_keep, back_low)

def rope_tables(positions):
    half_width = HEAD_WIDTH // 2
    frequency = ROPE_BASE ** (-(2.0 * jnp.arange(half_width, dtype=jnp.float32)) / HEAD_WIDTH)
    angle_table = positions.astype(jnp.float32)[:, None] * frequency[None, :]
    return (jnp.cos(angle_table)[:, None, :], jnp.sin(angle_table)[:, None, :])

def apply_rotation(heads, cosine_lookup, sine_lookup):
    half_width = heads.shape[-1] // 2
    first_half = heads[..., :half_width]
    second_half = heads[..., half_width:]
    return jnp.concatenate([first_half * cosine_lookup - second_half * sine_lookup, second_half * cosine_lookup + first_half * sine_lookup], axis=-1)

def attention(query_head_rows, key_head_rows, value_head_rows, length, window_now, global_here):
    rows_per_block = 512 if SEQUENCE_LENGTH % 512 == 0 else SEQUENCE_LENGTH
    group_count = QUERY_HEADS // KEY_VALUE_HEADS
    positions = jnp.arange(SEQUENCE_LENGTH, dtype=jnp.int32)
    key_global = jnp.any(positions[:, None] == global_here[None, :], axis=1)
    grouped_queries = query_head_rows.reshape(SEQUENCE_LENGTH // rows_per_block, rows_per_block, KEY_VALUE_HEADS, group_count, HEAD_WIDTH)
    starts = jnp.arange(SEQUENCE_LENGTH // rows_per_block, dtype=jnp.int32) * rows_per_block

    @jax.checkpoint
    def one_block(block_item):
        query_block, first_row = block_item
        rows_here = first_row + jnp.arange(rows_per_block, dtype=jnp.int32)
        row_global = jnp.any(rows_here[:, None] == global_here[None, :], axis=1)
        in_window = rows_here[:, None] - positions[None, :] < window_now
        allowed = (positions[None, :] <= rows_here[:, None]) & (positions[None, :] < length) & (in_window | row_global[:, None] | key_global[None, :])
        scores = jnp.einsum('igkd,jgd->gkij', query_block, key_head_rows, precision=PRECISE_DOT) * HEAD_WIDTH ** (-0.5)
        scores = low_back(scores)
        masked = jnp.where(allowed[None, None], scores, NEGATIVE_FILLER)
        row_top = lax.optimization_barrier(jnp.max(masked, axis=-1, keepdims=True))
        weights = jnp.where(allowed[None, None], jnp.exp(masked - row_top), 0.0)
        probs_low = lowered_input(weights / lax.optimization_barrier(jnp.sum(weights, axis=-1, keepdims=True)))
        block_out = jnp.einsum('gkij,jgd->igkd', probs_low, value_head_rows, precision=PRECISE_DOT)
        return block_out.reshape(rows_per_block, QUERY_HEADS * HEAD_WIDTH)
    block_outputs = lax.map(one_block, (grouped_queries, starts))
    return block_outputs.reshape(SEQUENCE_LENGTH, QUERY_HEADS * HEAD_WIDTH)

def layer_forward(rows_in, norm_attn, w_qkv, w_out, norm_ffn, w_gate, w_up, w_down, length, window_now, global_here):
    inv_attn = lax.rsqrt(lax.optimization_barrier(jnp.mean(rows_in * rows_in, axis=-1, keepdims=True)) + NORM_EPS)
    normed_attn = lowered_input(rows_in * inv_attn * norm_attn)
    packed_projection = low_back(jnp.dot(normed_attn, w_qkv, precision=PRECISE_DOT, preferred_element_type=jnp.float32))
    cosine_lookup, sine_lookup = rope_tables(jnp.arange(SEQUENCE_LENGTH, dtype=jnp.int32))
    query_head_rows = lowered_input(apply_rotation(packed_projection[:, :QUERY_HEADS * HEAD_WIDTH].reshape(SEQUENCE_LENGTH, QUERY_HEADS, HEAD_WIDTH), cosine_lookup, sine_lookup))
    key_head_rows = lowered_input(apply_rotation(packed_projection[:, QUERY_HEADS * HEAD_WIDTH:(QUERY_HEADS + KEY_VALUE_HEADS) * HEAD_WIDTH].reshape(SEQUENCE_LENGTH, KEY_VALUE_HEADS, HEAD_WIDTH), cosine_lookup, sine_lookup))
    value_head_rows = lowered_input(packed_projection[:, (QUERY_HEADS + KEY_VALUE_HEADS) * HEAD_WIDTH:].reshape(SEQUENCE_LENGTH, KEY_VALUE_HEADS, HEAD_WIDTH))
    attended_output = attention(query_head_rows, key_head_rows, value_head_rows, length, window_now, global_here)
    attended_low = low_back(lowered_input(attended_output))
    branch = low_back(jnp.dot(attended_low, w_out, precision=PRECISE_DOT, preferred_element_type=jnp.float32))
    middle = rows_in + branch
    inv_ffn = lax.rsqrt(lax.optimization_barrier(jnp.mean(middle * middle, axis=-1, keepdims=True)) + NORM_EPS)
    normed_ffn = lowered_input(middle * inv_ffn * norm_ffn)
    gate = low_back(jnp.dot(normed_ffn, w_gate.T, precision=PRECISE_DOT, preferred_element_type=jnp.float32))
    up_values = low_back(jnp.dot(normed_ffn, w_up.T, precision=PRECISE_DOT, preferred_element_type=jnp.float32))
    hidden = lowered_input(jax.nn.silu(gate) * up_values)
    return middle + jnp.dot(hidden, w_down, precision=PRECISE_DOT, preferred_element_type=jnp.float32)

def reference(tokens, cotangent, norm_attn, w_qkv, w_out, norm_ffn, w_gate, w_up, w_down, seq_len, window, global_pos):
    params = (norm_attn.astype(jnp.float32), w_qkv.astype(jnp.float32), w_out.astype(jnp.float32), norm_ffn.astype(jnp.float32), w_gate.astype(jnp.float32), w_up.astype(jnp.float32), w_down.astype(jnp.float32))

    def sequence_step(totals, sequence_item):
        rows_in, rows_grad, length, window_now, global_here = sequence_item

        def forward(rows_f, gain_one, matrix_qkv, matrix_out, gain_two, matrix_gate, matrix_up, matrix_down):
            return layer_forward(rows_f, gain_one, matrix_qkv, matrix_out, gain_two, matrix_gate, matrix_up, matrix_down, length, window_now, global_here)
        output, pullback = jax.vjp(forward, rows_in.astype(jnp.float32), params[0], params[1], params[2], params[3], params[4], params[5], params[6])
        gradients = pullback(rows_grad.astype(jnp.float32))
        totals = tuple((total_now + grad_now for total_now, grad_now in zip(totals, gradients[1:])))
        return (totals, (output.astype(jnp.bfloat16), gradients[0]))
    zeros_start = tuple((jnp.zeros(param_now.shape, jnp.float32) for param_now in params))
    totals, (layer_out, d_tokens) = lax.scan(sequence_step, zeros_start, (tokens, cotangent, seq_len, window, global_pos))
    return (layer_out, d_tokens, totals[0], totals[1], totals[2], totals[3], totals[4], totals[5], totals[6])
```

```python
import jax
import jax.numpy as jnp
from jax import lax
from jax.sharding import PartitionSpec as P

QUERY_HEADS = 16
KEY_VALUE_HEADS = 8
HEAD_WIDTH = 128
GROUP = QUERY_HEADS // KEY_VALUE_HEADS

NORM_EPS = 1e-05
NEGATIVE_FILLER = -1e30
ROPE_BASE = 1000000.0
BF16 = jnp.bfloat16
F32 = jnp.float32


def rope_tables(positions):
    half_width = HEAD_WIDTH // 2
    frequency = ROPE_BASE ** (-(2.0 * jnp.arange(half_width, dtype=F32)) / HEAD_WIDTH)
    angle_table = positions.astype(F32)[:, None] * frequency[None, :]
    return (jnp.cos(angle_table)[:, None, :], jnp.sin(angle_table)[:, None, :])


def apply_rotation(heads, cosine_lookup, sine_lookup):
    half_width = heads.shape[-1] // 2
    first_half = heads[..., :half_width]
    second_half = heads[..., half_width:]
    return jnp.concatenate(
        [
            first_half * cosine_lookup - second_half * sine_lookup,
            second_half * cosine_lookup + first_half * sine_lookup,
        ],
        axis=-1,
    )


def square():
    return lax.axis_size("ctx") == 4


def swap(x, bit):
    return lax.ppermute(x, "ctx", [(i, i ^ bit) for i in range(4)])


def block_order():
    if square():
        return lax.axis_index("ctx") ^ jnp.arange(4, dtype=jnp.int32)
    return jnp.arange(lax.axis_size("ctx"), dtype=jnp.int32)


def gather_ctx(x):
    if not square():
        return lax.all_gather(x, "ctx", axis=0)
    half = x.shape[-1] // 2
    first, second = x[..., :half], x[..., half:]
    first_1 = swap(first, 1)
    second_2 = swap(second, 2)
    first_23 = swap(jnp.stack([first, first_1]), 2)
    second_13 = swap(jnp.stack([second, second_2]), 1)
    return jnp.stack(
        [
            x,
            jnp.concatenate([first_1, second_13[0]], axis=-1),
            jnp.concatenate([first_23[0], second_2], axis=-1),
            jnp.concatenate([first_23[1], second_13[1]], axis=-1),
        ]
    )


def scatter_sum_ctx(x):
    if not square():
        return lax.psum_scatter(x, "ctx", scatter_dimension=0, tiled=False).astype(F32)
    half = x.shape[-1] // 2
    first, second = x[..., :half], x[..., half:]
    got_first = swap(jnp.stack([first[1], first[3]]), 1)
    got_second = swap(second[2:4], 2)
    first_2 = (first[2].astype(F32) + got_first[1].astype(F32)).astype(BF16)
    second_1 = (second[1].astype(F32) + got_second[1].astype(F32)).astype(BF16)
    last_first = swap(first_2, 2)
    last_second = swap(second_1, 1)
    return jnp.concatenate(
        [
            first[0].astype(F32) + got_first[0].astype(F32) + last_first.astype(F32),
            second[0].astype(F32) + got_second[0].astype(F32) + last_second.astype(F32),
        ],
        axis=-1,
    )


def absolute_order(blocks):
    if not square():
        return [blocks[i] for i in range(lax.axis_size("ctx"))]
    place = lax.axis_index("ctx")
    low, high = (place & 1) == 1, (place & 2) == 2
    a = [jnp.where(low, blocks[r ^ 1], blocks[r]) for r in range(4)]
    return [jnp.where(high, a[r ^ 2], a[r]) for r in range(4)]


def own_row_order(blocks):
    if not square():
        return blocks
    return [jnp.stack([blocks[s][r ^ s] for r in range(4)]) for s in range(4)]


def exchange_ctx(x):
    if not square():
        got = lax.all_to_all(x, "ctx", 0, 0, tiled=False)
        return [got[i] for i in range(lax.axis_size("ctx"))]
    order = block_order()
    parts = [lax.dynamic_index_in_dim(x, order[r], 0, keepdims=False) for r in range(4)]
    got = [parts[0]] + [swap(parts[r], r) for r in range(1, 4)]
    return absolute_order(got)


def local(
    tokens,
    cotangent,
    norm_attn,
    w_qkv,
    w_out,
    norm_ffn,
    w_gate,
    w_up,
    w_down,
    seq_len,
    window,
    global_pos,
):
    places = lax.axis_size("ctx")
    place = lax.axis_index("ctx")
    shards = lax.axis_size("fsdp")
    rows = tokens.shape[1]
    width = tokens.shape[2]
    count = places * rows
    kv_heads = KEY_VALUE_HEADS // places
    q_heads = kv_heads * GROUP
    q_cols = q_heads * HEAD_WIDTH
    kv_cols = kv_heads * HEAD_WIDTH
    q_all = QUERY_HEADS * HEAD_WIDTH
    kv_all = KEY_VALUE_HEADS * HEAD_WIDTH
    out_cols = width // places
    score_scale = HEAD_WIDTH ** (-0.5)
    length = seq_len[0]
    window_now = window[0]
    global_here = global_pos[0]
    x_own = tokens[0]
    cot_own = cotangent[0]

    qkv_mine = jnp.concatenate(
        [
            lax.dynamic_slice_in_dim(w_qkv, place * q_cols, q_cols, 1),
            lax.dynamic_slice_in_dim(w_qkv, q_all + place * kv_cols, kv_cols, 1),
            lax.dynamic_slice_in_dim(w_qkv, q_all + kv_all + place * kv_cols, kv_cols, 1),
        ],
        axis=1,
    )
    w_heads = lax.all_gather(qkv_mine, "fsdp", axis=0, tiled=True)
    gains = lax.all_gather(jnp.stack([norm_attn, norm_ffn]), "fsdp", axis=1, tiled=True)
    gain_attn = gains[0].astype(F32)
    gain_ffn = gains[1].astype(F32)
    x_seq = gather_ctx(x_own).reshape(count, width).astype(F32)
    out_mine = lax.dynamic_slice_in_dim(w_out, place * out_cols, out_cols, 1)
    out_gathered = lax.all_gather(out_mine, "fsdp", axis=0, tiled=True)
    w_rows = jnp.concatenate(
        exchange_ctx(out_gathered.reshape(places, q_cols, out_cols)), axis=1
    )
    cot_all = lax.all_gather(cot_own, "fsdp", axis=0, tiled=True)

    inv_attn = lax.rsqrt(jnp.mean(x_seq * x_seq, axis=-1, keepdims=True) + NORM_EPS)
    normed_low = (x_seq * inv_attn * gain_attn[None, :]).astype(BF16)
    packed = jnp.dot(normed_low, w_heads, preferred_element_type=F32)
    order = block_order()
    positions = (order[:, None] * rows + jnp.arange(rows, dtype=jnp.int32)[None, :]).reshape(count)
    cosine, sine = rope_tables(positions)
    queries = apply_rotation(
        packed[:, :q_cols].reshape(count, q_heads, HEAD_WIDTH), cosine, sine
    ).astype(BF16)
    queries = queries.reshape(count, kv_heads, GROUP, HEAD_WIDTH)
    keys = apply_rotation(
        packed[:, q_cols : q_cols + kv_cols].reshape(count, kv_heads, HEAD_WIDTH), cosine, sine
    ).astype(BF16)
    values = packed[:, q_cols + kv_cols :].reshape(count, kv_heads, HEAD_WIDTH).astype(BF16)
    is_global = jnp.any(positions[:, None] == global_here[None, :], axis=1)
    allowed = (
        (positions[None, :] <= positions[:, None])
        & (positions[None, :] < length)
        & (
            (positions[:, None] - positions[None, :] < window_now)
            | is_global[:, None]
            | is_global[None, :]
        )
    )
    scores = (
        jnp.einsum("igkd,jgd->gkij", queries, keys, preferred_element_type=F32) * score_scale
    )
    scores = jnp.where(allowed[None, None], scores, NEGATIVE_FILLER)
    top = jnp.max(scores, axis=-1, keepdims=True)
    weights = jnp.where(allowed[None, None], jnp.exp(scores - top), 0.0)
    probs = weights / jnp.sum(weights, axis=-1, keepdims=True)
    probs_low = probs.astype(BF16)
    attended = jnp.einsum(
        "gkij,jgd->igkd", probs_low, values, preferred_element_type=F32
    ).reshape(count, q_cols)
    attended_low = attended.astype(BF16)
    branch_part = jnp.dot(attended_low, w_rows, preferred_element_type=F32).astype(BF16)
    branch = scatter_sum_ctx(branch_part.reshape(places, rows, width))

    x_full = x_own.astype(F32)
    middle = x_full + branch
    inv_ffn = lax.rsqrt(jnp.mean(middle * middle, axis=-1, keepdims=True) + NORM_EPS)
    normed_ffn = middle * inv_ffn
    ffn_low = (normed_ffn * gain_ffn[None, :]).astype(BF16)
    ffn_all = lax.all_gather(ffn_low, "fsdp", axis=0, tiled=True)
    attended_all = jnp.concatenate(
        absolute_order(own_row_order(gather_ctx(attended_low.reshape(places, rows, q_cols)))), axis=-1
    ).reshape(count, q_all)
    gate = jnp.einsum("td,fd->tf", ffn_all, w_gate, preferred_element_type=F32)
    up = jnp.einsum("td,fd->tf", ffn_all, w_up, preferred_element_type=F32)
    d_hidden = jnp.einsum("td,fd->tf", cot_all, w_down, preferred_element_type=F32)
    sigmoid = jax.nn.sigmoid(gate)
    silu = gate * sigmoid
    hidden = (silu * up).astype(BF16)
    d_gate = (d_hidden * up * sigmoid * (1.0 + gate * (1.0 - sigmoid))).astype(BF16)
    d_up = (d_hidden * silu).astype(BF16)
    d_ffn_part = jnp.dot(d_gate, w_gate, preferred_element_type=F32) + jnp.dot(
        d_up, w_up, preferred_element_type=F32
    )
    d_ffn = lax.psum_scatter(
        d_ffn_part.astype(BF16), "fsdp", scatter_dimension=0, tiled=True
    ).astype(F32)
    ffn_part = jnp.dot(hidden, w_down, preferred_element_type=F32).astype(BF16)
    layer_out = middle + lax.psum_scatter(
        ffn_part, "fsdp", scatter_dimension=0, tiled=True
    ).astype(F32)
    grads_ffn = [
        lax.psum(
            jnp.einsum("tf,td->fd", a, b, preferred_element_type=F32).astype(BF16), "ctx"
        ).astype(F32)
        for a, b in ((hidden, cot_all), (d_gate, ffn_all), (d_up, ffn_all))
    ]

    scaled = d_ffn * gain_ffn[None, :]
    d_gain_ffn = jnp.sum(d_ffn * normed_ffn, axis=0)
    d_middle = cot_own.astype(F32) + inv_ffn * (
        scaled - normed_ffn * jnp.mean(scaled * normed_ffn, axis=-1, keepdims=True)
    )
    d_branch_own = d_middle.astype(BF16)
    d_branch = gather_ctx(d_branch_own).reshape(count, width)
    d_attended = jnp.einsum("te,fe->tf", d_branch, w_rows, preferred_element_type=F32).astype(BF16)
    d_att_heads = d_attended.reshape(count, kv_heads, GROUP, HEAD_WIDTH)
    delta = jnp.sum(
        d_attended.astype(F32).reshape(count, q_heads, HEAD_WIDTH)
        * attended.reshape(count, q_heads, HEAD_WIDTH),
        axis=-1,
    )
    delta = jnp.transpose(delta.reshape(count, kv_heads, GROUP), (1, 2, 0))
    d_probs = jnp.einsum("igkd,jgd->gkij", d_att_heads, values, preferred_element_type=F32)
    d_scores = (probs * (d_probs - delta[..., None])).astype(BF16)
    d_queries = score_scale * jnp.einsum(
        "gkij,jgd->igkd", d_scores, keys, preferred_element_type=F32
    )
    d_keys = score_scale * jnp.einsum(
        "gkij,igkd->jgd", d_scores, queries, preferred_element_type=F32
    )
    d_values = jnp.einsum("gkij,igkd->jgd", probs_low, d_att_heads, preferred_element_type=F32)
    d_packed = jnp.concatenate(
        [
            apply_rotation(
                d_queries.reshape(count, q_heads, HEAD_WIDTH), cosine, -sine
            ).reshape(count, q_cols),
            apply_rotation(d_keys, cosine, -sine).reshape(count, kv_cols),
            d_values.reshape(count, kv_cols),
        ],
        axis=-1,
    ).astype(BF16)
    d_attn_part = jnp.einsum("tc,dc->td", d_packed, w_heads, preferred_element_type=F32)
    d_attn = scatter_sum_ctx(d_attn_part.astype(BF16).reshape(places, rows, width))
    inv_own = lax.rsqrt(jnp.mean(x_full * x_full, axis=-1, keepdims=True) + NORM_EPS)
    normed_attn = x_full * inv_own
    scaled_attn = d_attn * gain_attn[None, :]
    d_tokens = d_middle + inv_own * (
        scaled_attn - normed_attn * jnp.mean(scaled_attn * normed_attn, axis=-1, keepdims=True)
    )

    d_out_cols = jnp.einsum(
        "tf,te->fe",
        attended_all,
        lax.dynamic_slice_in_dim(d_branch, place * out_cols, out_cols, 1),
        preferred_element_type=F32,
    ).astype(BF16)
    gain_cols = jnp.broadcast_to(d_gain_ffn.astype(BF16)[:, None], (width, 128))
    out_scattered = lax.psum_scatter(
        jnp.concatenate([d_out_cols, gain_cols], axis=1), "fsdp", scatter_dimension=0, tiled=True
    )
    out_blocks = absolute_order(gather_ctx(out_scattered))
    grad_out = jnp.concatenate([b[:, :out_cols] for b in out_blocks], axis=1).astype(F32)
    grad_gain_ffn = sum(b[:, out_cols].astype(F32) for b in out_blocks)
    d_heads = jnp.einsum("td,tc->dc", normed_low, d_packed, preferred_element_type=F32)
    heads_scattered = lax.psum_scatter(
        d_heads.astype(BF16), "fsdp", scatter_dimension=0, tiled=True
    )
    head_blocks = absolute_order(gather_ctx(heads_scattered))
    grad_qkv = jnp.concatenate(
        [b[:, :q_cols] for b in head_blocks]
        + [b[:, q_cols : q_cols + kv_cols] for b in head_blocks]
        + [b[:, q_cols + kv_cols :] for b in head_blocks],
        axis=1,
    ).astype(F32)
    grad_gain_attn = jnp.sum(grad_qkv * w_qkv.astype(F32), axis=1) / norm_attn.astype(F32)
    return (
        layer_out.astype(BF16)[None],
        d_tokens[None],
        grad_gain_attn,
        grad_qkv,
        grad_out,
        grad_gain_ffn,
        grads_ffn[1],
        grads_ffn[2],
        grads_ffn[0],
    )


def solution(mesh):
    return jax.shard_map(
        local,
        mesh=mesh,
        in_specs=(
            P("fsdp", "ctx", None),
            P("fsdp", "ctx", None),
            P("fsdp"),
            P("fsdp", None),
            P("fsdp", None),
            P("fsdp"),
            P("fsdp", None),
            P("fsdp", None),
            P("fsdp", None),
            P("fsdp"),
            P("fsdp"),
            P("fsdp", None),
        ),
        out_specs=(
            P("fsdp", "ctx", None),
            P("fsdp", "ctx", None),
            P("fsdp"),
            P("fsdp", None),
            P("fsdp", None),
            P("fsdp"),
            P("fsdp", None),
            P("fsdp", None),
            P("fsdp", None),
        ),
        check_vma=False,
    )
```

```python
import functools

import jax
import jax.numpy as jnp
from jax import lax
from jax.experimental import pallas as pl
from jax.experimental.pallas import tpu as pltpu
from jax.sharding import PartitionSpec as P

QUERY_HEADS = 16
KEY_VALUE_HEADS = 8
HEAD_WIDTH = 128
GROUP = QUERY_HEADS // KEY_VALUE_HEADS

NORM_EPS = 1e-05
NEGATIVE_FILLER = -1e30
ROPE_BASE = 1000000.0
LOG2_E = 1.4426950408889634
BF16 = jnp.bfloat16
F32 = jnp.float32


def rope_tables(positions):
    half_width = HEAD_WIDTH // 2
    frequency = ROPE_BASE ** (-(2.0 * jnp.arange(half_width, dtype=F32)) / HEAD_WIDTH)
    angle_table = positions.astype(F32)[:, None] * frequency[None, :]
    cosine, sine = jnp.cos(angle_table), jnp.sin(angle_table)
    return (
        jnp.concatenate([cosine, cosine], axis=1),
        jnp.concatenate([-sine, sine], axis=1),
    )


NT = (((1,), (1,)), ((), ()))
NN = (((1,), (0,)), ((), ()))
TN = (((0,), (0,)), ((), ()))
VMEM_LIMIT = 56 * 2**20


def product(a, b, dims):
    return lax.dot_general(a, b, dims, preferred_element_type=F32)


def pieces(length, most):
    size = most if length % most == 0 else length
    return [pl.ds(start, size) for start in range(0, length, size)]


def resident(shape):
    return pl.BlockSpec(shape, lambda i: (0,) * len(shape), pipeline_mode=pl.Buffered(1))


def kernel_params():
    return pltpu.CompilerParams(vmem_limit_bytes=VMEM_LIMIT)


def cost(us=0.3):
    return pl.CostEstimate(flops=int(us * 1e9), bytes_accessed=int(us * 3.69e6), transcendentals=0)


def anywhere(values):
    return [pl.BlockSpec(memory_space=pl.ANY)] * len(values)


def norm_project_kernel(blocks, count_in, *refs):
    parts, (gain_ref, weight_ref, normed_ref, out_ref) = refs[:count_in], refs[count_in:]

    @pl.when(pl.program_id(0) == 0)
    def _():
        gain = gain_ref[...]
        first_row = 0
        for block in blocks:
            pieces_of = []
            for i, lead in block:
                ref = parts[i]
                pieces_of.append((ref[...] if lead is None else ref[lead]).astype(F32))
            squares = sum(jnp.sum(p * p, axis=1, keepdims=True) for p in pieces_of)
            width = sum(p.shape[1] for p in pieces_of)
            inverse = lax.rsqrt(squares / width + NORM_EPS)
            column = 0
            for p in pieces_of:
                columns = pl.ds(column, p.shape[1])
                normed_ref[pl.ds(first_row, p.shape[0]), columns] = (
                    p * inverse * gain[:, column : column + p.shape[1]]
                ).astype(BF16)
                column += p.shape[1]
            first_row += pieces_of[0].shape[0]

    out_ref[...] = product(normed_ref[...], weight_ref[...], NN)


def norm_project(parts, blocks, gain, weights, columns):
    count = sum(parts[block[0][0]].shape[-2] for block in blocks)
    width = gain.shape[1]
    step = 256
    return pl.pallas_call(
        functools.partial(norm_project_kernel, blocks, len(parts)),
        out_shape=[
            jax.ShapeDtypeStruct((count, width), BF16),
            jax.ShapeDtypeStruct((count, columns), F32),
        ],
        grid=(columns // step,),
        in_specs=[resident(p.shape) for p in parts]
        + [resident((1, width)), pl.BlockSpec((width, step), lambda n: (0, n))],
        out_specs=[
            pl.BlockSpec((count, width), lambda n: (0, 0)),
            pl.BlockSpec((count, step), lambda n: (0, n)),
        ],
        compiler_params=kernel_params(),
        cost_estimate=cost(),
    )(*parts, gain, weights)


def hidden_kernel(x_ref, cot_ref, gate_up_ref, down_ref, *refs):
    hidden_ref, both_ref, hidden_t_ref, d_gate_t_ref, d_up_t_ref = refs[-5:]
    units = down_ref.shape[0]
    gate_up = product(x_ref[...], gate_up_ref[...], NT)
    d_hidden = product(cot_ref[...], down_ref[...], NT)
    gate, up = gate_up[:, :units], gate_up[:, units:]
    sigmoid = 1.0 / (1.0 + jnp.exp(-gate))
    silu = gate * sigmoid
    hidden = (silu * up).astype(BF16)
    d_gate = (d_hidden * up * (sigmoid + silu * (1.0 - sigmoid))).astype(BF16)
    d_up = (d_hidden * silu).astype(BF16)
    hidden_ref[...] = hidden
    both_ref[:, :units] = d_gate
    both_ref[:, units:] = d_up
    hidden_t_ref[...] = hidden.T
    d_gate_t_ref[...] = d_gate.T
    d_up_t_ref[...] = d_up.T


def hidden_grads(x, cot, gate_up, down, part, before=(), waits=()):
    count, width = x.shape
    units = down.shape[0] // 2
    block = 256
    rows_in = pl.BlockSpec((block, width), lambda i: (i, 0))
    once = pl.Buffered(1)
    transposed = pl.BlockSpec((units, block), lambda i: (0, i))
    return pl.pallas_call(
        hidden_kernel,
        out_shape=[
            jax.ShapeDtypeStruct((count, 2 * units), BF16),
            jax.ShapeDtypeStruct((count, 4 * units), BF16),
        ]
        + [jax.ShapeDtypeStruct((units, count), BF16)] * 3,
        grid=(count // block,),
        in_specs=[
            rows_in,
            rows_in,
            pl.BlockSpec((2 * units, width), lambda i: (part, 0), pipeline_mode=once),
            pl.BlockSpec((units, width), lambda i: (part, 0), pipeline_mode=once),
        ]
        + anywhere((*before, *waits)),
        out_specs=[
            pl.BlockSpec((block, units), lambda i: (i, part)),
            pl.BlockSpec((block, 2 * units), lambda i: (i, part)),
        ]
        + [transposed] * 3,
        input_output_aliases={4 + i: i for i in range(len(before))},
        compiler_params=kernel_params(),
        cost_estimate=cost(),
    )(x, cot, gate_up, down, *before, *waits)


def rows_product_kernel(a_ref, w_ref, *refs):
    out_ref = refs[-1]
    for rows in pieces(out_ref.shape[0], 512):
        out_ref[rows, :] = product(a_ref[rows, :], w_ref[...], NN).astype(BF16)


def rows_product(a, w, waits=(), us=0.3):
    count, depth = a.shape
    width = w.shape[1]
    block = 512
    return pl.pallas_call(
        rows_product_kernel,
        out_shape=jax.ShapeDtypeStruct((count, width), BF16),
        grid=(width // block,),
        in_specs=[resident((count, depth)), pl.BlockSpec((depth, block), lambda n: (0, n))]
        + anywhere(waits),
        out_specs=pl.BlockSpec((count, block), lambda n: (0, n)),
        compiler_params=kernel_params(),
        cost_estimate=cost(us),
    )(a, w, *waits)


def weight_grad_kernel(a_ref, b_ref, *refs):
    first_ref, upper_ref, lower_ref = refs[-3:]
    n = pl.program_id(0)
    height = upper_ref.shape[0]
    result = product(a_ref[...], b_ref[...], NN).astype(BF16)

    @pl.when(n < 2)
    def _():
        first_ref[0] = result[:height]
        first_ref[1] = result[height:]

    @pl.when(n >= 2)
    def _():
        upper_ref[...] = result[:height]
        lower_ref[...] = result[height:]


def weight_grad(a, b, waits=(), us=0.3):
    units, count = a.shape
    width = b.shape[1]
    height, half, block = units // 2, width // 2, width // 4
    lone = pl.BlockSpec((height, block), lambda n: (0, jnp.maximum(n - 2, 0)))
    return pl.pallas_call(
        weight_grad_kernel,
        out_shape=[
            jax.ShapeDtypeStruct((2, height, half), BF16),
            jax.ShapeDtypeStruct((height, half), BF16),
            jax.ShapeDtypeStruct((height, half), BF16),
        ],
        grid=(4,),
        in_specs=[
            resident((units, count)),
            pl.BlockSpec((count, block), lambda n: (0, n)),
        ]
        + anywhere(waits),
        out_specs=[
            pl.BlockSpec((2, height, block), lambda n: (0, 0, jnp.minimum(n, 1))),
            lone,
            lone,
        ],
        compiler_params=kernel_params(),
        cost_estimate=cost(us),
    )(a, b, *waits)


def parts_kernel(dims, lhs_ref, rhs_ref, first_sent, first_kept, second_sent, second_kept):
    n = pl.program_id(0)
    rows = first_sent.shape[1]
    result = product(lhs_ref[...], rhs_ref[...], dims).astype(BF16)
    blocks = [result[r * rows : (r + 1) * rows] for r in range(4)]

    @pl.when(n < 2)
    def _():
        first_kept[0], first_sent[0], first_kept[1], first_sent[1] = blocks

    @pl.when(n >= 2)
    def _():
        second_kept[0], second_kept[1], second_sent[0], second_sent[1] = blocks


def product_in_parts(lhs, rhs, dims, width):
    count, depth = lhs.shape
    if not square():
        if dims == NT:
            rhs = rhs[:, :depth]
        return product(lhs, rhs, dims).astype(BF16).reshape(lax.axis_size("ctx"), -1, width)
    block = width // 4
    if dims == NT:
        rhs_spec = pl.BlockSpec((block, depth), lambda n: (n, 0))
    else:
        rhs_spec = pl.BlockSpec((depth, block), lambda n: (0, n))
    shape = (2, count // 4, width // 2)
    first = pl.BlockSpec((*shape[:2], block), lambda n: (0, 0, jnp.minimum(n, 1)))
    second = pl.BlockSpec((*shape[:2], block), lambda n: (0, 0, jnp.maximum(n - 2, 0)))
    return pl.pallas_call(
        functools.partial(parts_kernel, dims),
        out_shape=[jax.ShapeDtypeStruct(shape, BF16)] * 4,
        grid=(4,),
        in_specs=[resident((count, depth)), rhs_spec],
        out_specs=[first, first, second, second],
        compiler_params=kernel_params(),
        cost_estimate=cost(),
    )(lhs, rhs)


def rows_grad_kernel(terms, *refs):
    out_ref = refs[-1]
    column = 0
    for i in range(terms):
        columns = pl.ds(column, refs[terms + i].shape[1])
        out_ref[:, columns] = product(refs[i][...], refs[terms + i][...], TN).astype(BF16)
        column += refs[terms + i].shape[1]
    out_ref[:, column:] = refs[2 * terms][...]


def rows_grad(terms, beside, waits=()):
    count, width = terms[0][0].shape
    block = 512
    total = sum(b.shape[1] for _, b in terms) + beside.shape[1]
    return pl.pallas_call(
        functools.partial(rows_grad_kernel, len(terms)),
        out_shape=jax.ShapeDtypeStruct((width, total), BF16),
        grid=(width // block,),
        in_specs=[pl.BlockSpec((count, block), lambda m: (0, m))] * len(terms)
        + [resident(b.shape) for _, b in terms]
        + [pl.BlockSpec((block, beside.shape[1]), lambda m: (m, 0))]
        + anywhere(waits),
        out_specs=pl.BlockSpec((block, total), lambda m: (m, 0)),
        compiler_params=kernel_params(),
        cost_estimate=cost(),
    )(*[a for a, _ in terms], *[b for _, b in terms], beside, *waits)


def turned(x, cosine, sine):
    return x * cosine + pltpu.roll(x, HEAD_WIDTH // 2, 1) * sine


def attend_kernel(
    query_in, key_in, value_in, cos_ref, sin_ref, bias_ref, query_ref, key_ref, value_ref, probs_ref, out_ref
):
    scale = HEAD_WIDTH ** (-0.5) * LOG2_E
    key = turned(key_in[...], cos_ref[...], sin_ref[...]).astype(BF16)
    value = value_in[...].astype(BF16)
    key_ref[...] = key
    value_ref[...] = value
    for h in range(GROUP):
        head = pl.ds(h * HEAD_WIDTH, HEAD_WIDTH)
        for rows in pieces(query_in.shape[0], 256):
            query = turned(query_in[rows, head], cos_ref[rows, :], sin_ref[rows, :]).astype(BF16)
            query_ref[rows, head] = query
            scores = product(query, key, NT) * scale + bias_ref[rows, :]
            weights = jnp.exp2(scores - jnp.max(scores, axis=1, keepdims=True))
            probs = (weights * (1.0 / jnp.sum(weights, axis=1, keepdims=True))).astype(BF16)
            probs_ref[h, rows, :] = probs
            out_ref[rows, head] = product(probs, value, NN).astype(BF16)


def attend(packed, cosine, sine, bias, kv_heads):
    count = packed.shape[0]
    wide, narrow = GROUP * HEAD_WIDTH, HEAD_WIDTH
    q_heads = kv_heads * GROUP

    def column(width, first):
        return pl.BlockSpec((count, width), lambda g: (0, first + g))

    def sized(*shape):
        return jax.ShapeDtypeStruct(shape, BF16)

    return pl.pallas_call(
        attend_kernel,
        out_shape=[
            sized(count, kv_heads * wide),
            sized(count, kv_heads * narrow),
            sized(count, kv_heads * narrow),
            sized(q_heads, count, count),
            sized(count, kv_heads * wide),
        ],
        grid=(kv_heads,),
        in_specs=[
            column(wide, 0),
            column(narrow, q_heads),
            column(narrow, q_heads + kv_heads),
            resident((count, HEAD_WIDTH)),
            resident((count, HEAD_WIDTH)),
            resident((count, count)),
        ],
        out_specs=[
            column(wide, 0),
            column(narrow, 0),
            column(narrow, 0),
            pl.BlockSpec((GROUP, count, count), lambda g: (g, 0, 0)),
            column(wide, 0),
        ],
        compiler_params=kernel_params(),
        cost_estimate=cost(),
    )(packed, packed, packed, cosine, sine, bias)


def attend_back_kernel(
    query_ref, key_ref, value_ref, probs_ref, d_out_ref, out_ref, cos_ref, sin_ref, *refs
):
    packed_ref = refs[-1]
    g = pl.program_id(0)
    kv_heads = pl.num_programs(0)
    scale = HEAD_WIDTH ** (-0.5)
    key, value = key_ref[...], value_ref[...]
    d_key = d_value = None
    for h in range(GROUP):
        head = pl.ds(h * HEAD_WIDTH, HEAD_WIDTH)
        for rows in pieces(query_ref.shape[0], 256):
            d_out = d_out_ref[rows, head]
            delta = jnp.sum(
                d_out.astype(F32) * out_ref[rows, head].astype(F32), axis=1, keepdims=True
            )
            probs = probs_ref[h, rows, :]
            d_scores = (probs.astype(F32) * (product(d_out, value, NT) - delta)).astype(BF16)
            d_query = turned(
                product(d_scores, key, NN) * scale, cos_ref[rows, :], -sin_ref[rows, :]
            )
            place = pl.multiple_of((g * GROUP + h) * HEAD_WIDTH, HEAD_WIDTH)
            packed_ref[rows, pl.ds(place, HEAD_WIDTH)] = d_query.astype(BF16)
            d_key_here = product(d_scores, query_ref[rows, head], TN)
            d_value_here = product(probs, d_out, TN)
            d_key = d_key_here if d_key is None else d_key + d_key_here
            d_value = d_value_here if d_value is None else d_value + d_value_here
    place = pl.multiple_of((kv_heads * GROUP + g) * HEAD_WIDTH, HEAD_WIDTH)
    packed_ref[:, pl.ds(place, HEAD_WIDTH)] = turned(
        d_key * scale, cos_ref[...], -sin_ref[...]
    ).astype(BF16)
    place = pl.multiple_of((kv_heads * (GROUP + 1) + g) * HEAD_WIDTH, HEAD_WIDTH)
    packed_ref[:, pl.ds(place, HEAD_WIDTH)] = d_value.astype(BF16)


def attend_back(queries, keys, values, probs, d_out, out, cosine, sine, waits=()):
    count = queries.shape[0]
    kv_heads = keys.shape[1] // HEAD_WIDTH
    wide, narrow = GROUP * HEAD_WIDTH, HEAD_WIDTH

    def column(width):
        return pl.BlockSpec((count, width), lambda g: (0, g))

    packed_shape = (count, kv_heads * (GROUP + 2) * HEAD_WIDTH)
    return pl.pallas_call(
        attend_back_kernel,
        out_shape=jax.ShapeDtypeStruct(packed_shape, BF16),
        grid=(kv_heads,),
        in_specs=[
            column(wide),
            column(narrow),
            column(narrow),
            pl.BlockSpec((GROUP, count, count), lambda g: (g, 0, 0)),
            column(wide),
            column(wide),
            resident((count, HEAD_WIDTH)),
            resident((count, HEAD_WIDTH)),
        ]
        + anywhere(waits),
        out_specs=pl.BlockSpec(packed_shape, lambda g: (0, 0)),
        compiler_params=kernel_params(),
        cost_estimate=cost(),
    )(queries, keys, values, probs, d_out, out, cosine, sine, *waits)


def square():
    return lax.axis_size("ctx") == 4


def swap(x, bit):
    return lax.ppermute(x, "ctx", [(i, i ^ bit) for i in range(4)])


def block_order():
    if square():
        return lax.axis_index("ctx") ^ jnp.arange(4, dtype=jnp.int32)
    return jnp.arange(lax.axis_size("ctx"), dtype=jnp.int32)


def gather_parts(x, *others):
    if not square():
        return [lax.all_gather(x, "ctx", axis=0, tiled=True)], [[(0, None)]]
    half = -(-x.shape[-1] // 256) * 128
    first, second = x[..., :half], x[..., half:]
    first_1 = swap(first, 1)
    second_2 = swap(second, 2)
    first_01, second_02 = jnp.stack([first, first_1]), jnp.stack([second, second_2])
    if others:
        first_01, second_02 = after(first_01, *others), after(second_02, *others)
    first_23 = swap(first_01, 2)
    second_13 = swap(second_02, 1)
    blocks = [[(0, None)], [(1, None), (4, 0)], [(3, 0), (2, None)], [(3, 1), (4, 1)]]
    return [x, first_1, second_2, first_23, second_13], blocks


def gather_ctx(x):
    if not square():
        return lax.all_gather(x, "ctx", axis=0)
    parts, blocks = gather_parts(x)
    return jnp.stack(
        [
            jnp.concatenate([parts[i] if lead is None else parts[i][lead] for i, lead in block], axis=-1)
            for block in blocks
        ]
    )


def scatter_sum_ctx(parts):
    if not square():
        return lax.psum_scatter(parts, "ctx", scatter_dimension=0, tiled=False).astype(F32)
    first_sent, first_kept, second_sent, second_kept = parts
    got_first = swap(first_sent, 1)
    got_second = swap(second_sent, 2)
    last_first = swap(sum_low(first_kept[1], got_first[1]), 2)
    last_second = swap(sum_low(second_kept[1], got_second[1]), 1)
    return jnp.concatenate(
        [
            first_kept[0].astype(F32) + got_first[0].astype(F32) + last_first.astype(F32),
            second_kept[0].astype(F32) + got_second[0].astype(F32) + last_second.astype(F32),
        ],
        axis=-1,
    )


def absolute_order(blocks):
    if not square():
        return [blocks[i] for i in range(lax.axis_size("ctx"))]
    place = lax.axis_index("ctx")
    low, high = (place & 1) == 1, (place & 2) == 2
    a = [jnp.where(low, blocks[r ^ 1], blocks[r]) for r in range(4)]
    return [jnp.where(high, a[r ^ 2], a[r]) for r in range(4)]


def own_row_order(blocks):
    if not square():
        return blocks
    return [jnp.stack([blocks[s][r ^ s] for r in range(4)]) for s in range(4)]


def exchange_ctx(x):
    if not square():
        got = lax.all_to_all(x, "ctx", 0, 0, tiled=False)
        return [got[i] for i in range(lax.axis_size("ctx"))]
    order = block_order()
    parts = [lax.dynamic_index_in_dim(x, order[r], 0, keepdims=False) for r in range(4)]
    got = [parts[0]] + [swap(parts[r], r) for r in range(1, 4)]
    return absolute_order(got)


def nothing_kernel(*refs):
    del refs


def after(x, *others):
    if not square():
        return x
    return pl.pallas_call(
        nothing_kernel,
        out_shape=jax.ShapeDtypeStruct(x.shape, x.dtype),
        in_specs=anywhere((x, *others)),
        out_specs=anywhere((x,))[0],
        input_output_aliases={0: 0},
        cost_estimate=pl.CostEstimate(flops=0, bytes_accessed=0, transcendentals=0),
    )(x, *others)


def unit_halves(*weights):
    units = weights[0].shape[0]
    if not square():
        halves = [[w[: units // 2], w[units // 2 :]] for w in weights]
    else:
        place = lax.axis_index("ctx")
        blocks = [w.reshape(4, units // 4, w.shape[1]) for w in weights]

        def half(w, order):
            return jnp.concatenate(
                [lax.dynamic_index_in_dim(w, place ^ r, 0, keepdims=False) for r in order]
            )

        halves = [[half(w, (1, 3)), half(w, (2, 0))] for w in blocks]
    return jnp.concatenate([h[i] for i in range(2) for h in halves])


def lay_heads_kernel(blocks, sizes, place_ref, weight_ref, gain_ref, *refs):
    parts, (qkv_ref, out_ref, gain_attn_ref, gain_ffn_ref) = refs[:-4], refs[-4:]
    q_cols, kv_cols, out_cols, places = sizes
    head_cols = q_cols + 2 * kv_cols
    gain_attn = gain_ffn = 0.0
    for r, block in enumerate(blocks):
        place = place_ref[r]
        rows = jnp.concatenate(
            [parts[i][...] if lead is None else parts[i][lead] for i, lead in block], axis=1
        ).astype(F32)
        first = 0
        for width, start in (
            (q_cols, 0),
            (kv_cols, q_cols * places),
            (kv_cols, (q_cols + kv_cols) * places),
        ):
            columns = pl.ds(pl.multiple_of(start + place * width, 128), width)
            piece = rows[:, first : first + width]
            qkv_ref[:, columns] = piece
            gain_attn += jnp.sum(piece * weight_ref[:, columns].astype(F32), axis=1, keepdims=True)
            first += width
        columns = pl.ds(pl.multiple_of(place * out_cols, 128), out_cols)
        out_ref[:, columns] = rows[:, head_cols : head_cols + out_cols]
        gain_ffn += rows[:, head_cols + out_cols : head_cols + out_cols + 1]
    gain_attn_ref[...] = gain_attn / gain_ref[...]
    gain_ffn_ref[...] = gain_ffn


def lay_heads(parts, blocks, sizes, w_qkv, norm_attn, waits):
    rows, qkv_cols = w_qkv.shape
    q_cols, kv_cols, out_cols, places = sizes
    whole = pl.BlockSpec(memory_space=pltpu.VMEM)
    column = jax.ShapeDtypeStruct((rows, 1), F32)
    return pl.pallas_call(
        functools.partial(lay_heads_kernel, blocks, sizes),
        out_shape=[
            jax.ShapeDtypeStruct((rows, qkv_cols), F32),
            jax.ShapeDtypeStruct((rows, out_cols * places), F32),
            column,
            column,
        ],
        in_specs=[pl.BlockSpec(memory_space=pltpu.SMEM)]
        + [whole] * (2 + len(parts))
        + anywhere(waits),
        out_specs=[whole] * 4,
        compiler_params=kernel_params(),
        cost_estimate=cost(),
    )(block_order(), w_qkv, norm_attn.astype(F32)[:, None], *parts, *waits)


def lay_out_kernel(place_ref, first_own, first_got, second_own, second_got, *refs):
    out_ref = refs[-1]
    step = pl.program_id(0)
    for i, block in enumerate((first_own, first_got, second_own, second_got)):

        @pl.when(step // 2 == i)
        def _(block=block):
            out_ref[...] = block[0].astype(F32)


def lay_out(first_own, first_got, second_own, second_got, waits, us):
    _, height, half = first_own.shape
    places = lax.axis_index("ctx") ^ jnp.array([0, 2, 1, 3, 0, 1, 2, 3], jnp.int32)

    def block_of(i):
        return pl.BlockSpec(
            (1, height, half), lambda g, where: (jnp.clip(g - 2 * i, 0, 1), 0, 0)
        )

    return pl.pallas_call(
        lay_out_kernel,
        out_shape=jax.ShapeDtypeStruct((4 * height, 2 * half), F32),
        grid_spec=pltpu.PrefetchScalarGridSpec(
            num_scalar_prefetch=1,
            grid=(8,),
            in_specs=[block_of(i) for i in range(4)] + anywhere(waits),
            out_specs=pl.BlockSpec((height, half), lambda g, where: (where[g], g // 4)),
        ),
        compiler_params=pltpu.CompilerParams(vmem_limit_bytes=32 * 2**20),
        cost_estimate=cost(us),
    )(places, first_own, first_got, second_own, second_got, *waits)


def sum_low(*terms):
    return sum(t.astype(F32) for t in terms).astype(BF16)


class SumCtx:
    def start_first(self, part):
        self.upper = part
        if not square():
            return
        self.got_first = swap(part[0], 1)
        self.got_third = swap(part[2], 2)

    def start_second(self, part):
        self.lower = part
        if not square():
            blocks = []
            for first, upper, lower in (self.upper, part):
                second = jnp.stack([upper, lower])
                blocks.append(jnp.concatenate([first, second], axis=-1))
            whole = jnp.concatenate(blocks)
            self.whole = lax.psum(whole.reshape(-1, whole.shape[-1]), "ctx").astype(F32)
            return
        self.got_second = swap(part[1], 2)

    def arrived(self, second=False):
        if not square():
            return ()
        return (self.got_second,) if second else (self.got_first, self.got_third)

    def step_2(self, *others):
        if not square():
            return ()
        first = sum_low(self.lower[0][0], self.got_first[1])
        second = sum_low(self.upper[1], self.got_third)
        self.last_first = swap(after(first, *others) if others else first, 2)
        self.last_second = swap(after(second, *others) if others else second, 1)
        return (self.last_first, self.last_second)

    def step_3(self, *others):
        if not square():
            return ()
        self.first = sum_low(self.lower[0][1], self.got_first[0], self.last_first)
        self.second = sum_low(self.lower[2], self.got_second, self.last_second)
        if others:
            self.first = after(self.first, *others)
            self.second = after(self.second, *others)
        self.first_2 = swap(self.first, 2)
        self.second_1 = swap(self.second, 1)
        return (self.first_2, self.second_1)

    def step_4(self, *others):
        if not square():
            return ()
        self.first_02 = jnp.stack([self.first, self.first_2])
        self.second_01 = jnp.stack([self.second, self.second_1])
        if others:
            self.first_02 = after(self.first_02, *others)
            self.second_01 = after(self.second_01, *others)
        self.first_13 = swap(self.first_02, 1)
        self.second_23 = swap(self.second_01, 2)
        return (self.first_13, self.second_23)

    def result(self, waits=(), us=0.3):
        if not square():
            return self.whole
        return lay_out(self.first_02, self.first_13, self.second_01, self.second_23, waits, us)


def local(
    tokens,
    cotangent,
    norm_attn,
    w_qkv,
    w_out,
    norm_ffn,
    w_gate,
    w_up,
    w_down,
    seq_len,
    window,
    global_pos,
):
    places = lax.axis_size("ctx")
    place = lax.axis_index("ctx")
    shards = lax.axis_size("fsdp")
    rows = tokens.shape[1]
    width = tokens.shape[2]
    count = places * rows
    kv_heads = KEY_VALUE_HEADS // places
    q_heads = kv_heads * GROUP
    q_cols = q_heads * HEAD_WIDTH
    kv_cols = kv_heads * HEAD_WIDTH
    q_all = QUERY_HEADS * HEAD_WIDTH
    kv_all = KEY_VALUE_HEADS * HEAD_WIDTH
    out_cols = width // places
    length = seq_len[0]
    window_now = window[0]
    global_here = global_pos[0]
    x_own = tokens[0]
    cot_own = cotangent[0]

    head_cols = q_cols + 2 * kv_cols
    weights_mine = jnp.concatenate(
        [
            lax.dynamic_slice_in_dim(w_qkv, place * q_cols, q_cols, 1),
            lax.dynamic_slice_in_dim(w_qkv, q_all + place * kv_cols, kv_cols, 1),
            lax.dynamic_slice_in_dim(w_qkv, q_all + kv_all + place * kv_cols, kv_cols, 1),
            lax.dynamic_slice_in_dim(w_out, place * out_cols, out_cols, 1),
        ],
        axis=1,
    )
    weights = lax.all_gather(weights_mine, "fsdp", axis=0, tiled=True)
    gains = lax.all_gather(jnp.stack([norm_attn, norm_ffn]), "fsdp", axis=1, tiled=True)
    gain_attn = gains[0].astype(F32)
    gain_ffn = gains[1].astype(F32)
    x_parts, x_blocks = gather_parts(x_own, gains)
    cot_all = lax.all_gather(after(cot_own, *x_parts[-2:]), "fsdp", axis=0, tiled=True)
    gate_up = unit_halves(w_gate, w_up)
    down = unit_halves(w_down)
    w_rows = jnp.concatenate(
        exchange_ctx(weights[:, head_cols:].reshape(places, q_cols, out_cols)), axis=1
    )

    normed_low, packed = norm_project(x_parts, x_blocks, gain_attn[None, :], weights, head_cols)
    order = block_order()
    positions = (order[:, None] * rows + jnp.arange(rows, dtype=jnp.int32)[None, :]).reshape(count)
    cosine, sine = rope_tables(positions)
    is_global = jnp.any(positions[:, None] == global_here[None, :], axis=1)
    allowed = (
        (positions[None, :] <= positions[:, None])
        & (positions[None, :] < length)
        & (
            (positions[:, None] - positions[None, :] < window_now)
            | is_global[:, None]
            | is_global[None, :]
        )
    )
    bias = jnp.where(allowed, 0.0, NEGATIVE_FILLER)
    queries, keys, values, probs, attended_low = attend(packed, cosine, sine, bias, kv_heads)
    branch = scatter_sum_ctx(product_in_parts(attended_low, w_rows, NN, width))

    x_full = x_own.astype(F32)
    middle = x_full + branch
    inv_ffn = lax.rsqrt(jnp.mean(middle * middle, axis=-1, keepdims=True) + NORM_EPS)
    normed_ffn = middle * inv_ffn
    ffn_low = (normed_ffn * gain_ffn[None, :]).astype(BF16)
    ffn_all = lax.all_gather(after(ffn_low, cot_all), "fsdp", axis=0, tiled=True)
    attended_all = jnp.concatenate(
        absolute_order(own_row_order(gather_ctx(attended_low.reshape(places, rows, q_cols)))), axis=-1
    ).reshape(count, q_all)
    sum_down, sum_gate, sum_up = SumCtx(), SumCtx(), SumCtx()
    hidden, d_both, *first_t = hidden_grads(ffn_all, cot_all, gate_up, down, 0, (), (attended_all,))
    down_a = weight_grad(first_t[0], cot_all)
    sum_down.start_first(down_a)
    hidden, d_both, *second_t = hidden_grads(
        ffn_all, cot_all, gate_up, down, 1, (hidden, d_both), down_a
    )
    gate_a = weight_grad(first_t[1], ffn_all, (second_t[0], *sum_down.arrived()))
    sum_gate.start_first(gate_a)
    d_ffn_part = rows_product(d_both, gate_up, gate_a)
    d_ffn = lax.psum_scatter(d_ffn_part, "fsdp", scatter_dimension=0, tiled=True)
    down_b = weight_grad(second_t[0], cot_all, (d_ffn_part, *sum_gate.arrived()))
    sum_down.start_second(down_b)
    down_2 = sum_down.step_2()
    up_a = weight_grad(first_t[2], ffn_all, down_b, 300)
    sum_up.start_first(up_a)
    ffn_part = rows_product(hidden, down, (*up_a, *down_2, *sum_down.arrived(True)), 300)
    gate_b = weight_grad(second_t[1], ffn_all, (ffn_part, *sum_up.arrived()), 300)
    sum_gate.start_second(gate_b)
    gate_2 = sum_gate.step_2()
    down_3 = sum_down.step_3()
    up_b = weight_grad(second_t[2], ffn_all, gate_b, 300)
    sum_up.start_second(up_b)
    d_ffn = after(d_ffn, *down_3, *gate_2)
    ffn_sum = lax.psum_scatter(ffn_part, "fsdp", scatter_dimension=0, tiled=True)
    layer_out = middle + ffn_sum.astype(F32)

    d_ffn = d_ffn.astype(F32)
    scaled = d_ffn * gain_ffn[None, :]
    d_gain_ffn = jnp.sum(d_ffn * normed_ffn, axis=0)
    d_middle = cot_own.astype(F32) + inv_ffn * (
        scaled - normed_ffn * jnp.mean(scaled * normed_ffn, axis=-1, keepdims=True)
    )
    d_branch_own = d_middle.astype(BF16)
    d_branch = gather_ctx(d_branch_own).reshape(count, width)
    d_attended = jnp.einsum("te,fe->tf", d_branch, w_rows, preferred_element_type=F32).astype(BF16)
    up_2 = sum_up.step_2(d_branch)
    gate_3 = sum_gate.step_3(d_branch)
    down_4 = sum_down.step_4(d_branch)
    up_3 = sum_up.step_3()
    d_packed = attend_back(
        queries, keys, values, probs, d_attended, attended_low, cosine, sine
    )
    d_weights = rows_grad(
        [
            (normed_low, d_packed),
            (attended_all, lax.dynamic_slice_in_dim(d_branch, place * out_cols, out_cols, 1)),
        ],
        jnp.broadcast_to(d_gain_ffn.astype(BF16)[:, None], (width, 128)),
    )
    d_weights = after(d_weights, ffn_sum)
    d_attn_parts = product_in_parts(after(d_packed, d_weights, *up_2, *gate_3), weights, NT, width)
    scattered = lax.psum_scatter(d_weights, "fsdp", scatter_dimension=0, tiled=True)
    d_attn = scatter_sum_ctx(d_attn_parts)
    d_attn = after(d_attn, *down_4, *up_3)
    sum_gate.step_4(d_weights)
    sum_up.step_4(d_weights)
    inv_own = lax.rsqrt(jnp.mean(x_full * x_full, axis=-1, keepdims=True) + NORM_EPS)
    normed_attn = x_full * inv_own
    scaled_attn = d_attn * gain_attn[None, :]
    d_tokens = d_middle + inv_own * (
        scaled_attn - normed_attn * jnp.mean(scaled_attn * normed_attn, axis=-1, keepdims=True)
    )

    grad_down = sum_down.result(d_attn_parts, 300)
    parts, blocks = gather_parts(after(scattered, grad_down))
    if not square():
        rows_here = scattered.shape[0]
        parts = [parts[0].reshape(places, rows_here, -1)]
        blocks = [[(0, i)] for i in range(places)]
    grad_up = sum_up.result()
    grad_qkv, grad_out, grad_gain_attn, grad_gain_ffn = lay_heads(
        parts, blocks, (q_cols, kv_cols, out_cols, places), w_qkv, norm_attn, (grad_up,)
    )
    return (
        layer_out.astype(BF16)[None],
        d_tokens[None],
        grad_gain_attn[:, 0],
        grad_qkv,
        grad_out,
        grad_gain_ffn[:, 0],
        sum_gate.result(),
        grad_up,
        grad_down,
    )


def solution(mesh):
    return jax.shard_map(
        local,
        mesh=mesh,
        in_specs=(
            P("fsdp", "ctx", None),
            P("fsdp", "ctx", None),
            P("fsdp"),
            P("fsdp", None),
            P("fsdp", None),
            P("fsdp"),
            P("fsdp", None),
            P("fsdp", None),
            P("fsdp", None),
            P("fsdp"),
            P("fsdp"),
            P("fsdp", None),
        ),
        out_specs=(
            P("fsdp", "ctx", None),
            P("fsdp", "ctx", None),
            P("fsdp"),
            P("fsdp", None),
            P("fsdp", None),
            P("fsdp"),
            P("fsdp", None),
            P("fsdp", None),
            P("fsdp", None),
        ),
        check_vma=False,
    )
```

```python
import functools

import jax
import jax.numpy as jnp
from jax import lax
from jax.experimental import pallas as pl
from jax.experimental.pallas import tpu as pltpu
from jax.sharding import PartitionSpec as P

QUERY_HEADS = 16
KEY_VALUE_HEADS = 8
HEAD_WIDTH = 128
GROUP = QUERY_HEADS // KEY_VALUE_HEADS

NORM_EPS = 1e-05
NEGATIVE_FILLER = -1e30
ROPE_BASE = 1000000.0
LOG2_E = 1.4426950408889634
BF16 = jnp.bfloat16
F32 = jnp.float32


def rope_tables(positions):
    half_width = HEAD_WIDTH // 2
    frequency = ROPE_BASE ** (-(2.0 * jnp.arange(half_width, dtype=F32)) / HEAD_WIDTH)
    angle_table = positions.astype(F32)[:, None] * frequency[None, :]
    cosine, sine = jnp.cos(angle_table), jnp.sin(angle_table)
    return (
        jnp.concatenate([cosine, cosine], axis=1),
        jnp.concatenate([-sine, sine], axis=1),
    )


NT = (((1,), (1,)), ((), ()))
NN = (((1,), (0,)), ((), ()))
TN = (((0,), (0,)), ((), ()))
VMEM_LIMIT = 56 * 2**20


def product(a, b, dims):
    return lax.dot_general(a, b, dims, preferred_element_type=F32)


def pieces(length, most):
    size = most if length % most == 0 else length
    return [pl.ds(start, size) for start in range(0, length, size)]


def resident(shape):
    return pl.BlockSpec(shape, lambda i: (0,) * len(shape), pipeline_mode=pl.Buffered(1))


def kernel_params():
    return pltpu.CompilerParams(vmem_limit_bytes=VMEM_LIMIT)


PLAN = {'c_k0': 0.3, 'c_ha': 0.3, 'c_da': 0.3, 'c_hb': 0.3, 'c_ga': 0.3, 'c_df': 0.3, 'c_db': 0.3, 'c_ua': 300, 'c_ou': 300, 'c_gb': 300, 'c_ub': 300, 'c_op': 0.3, 'c_at': 0.3, 'c_k4': 0.3, 'c_rg': 0.3, 'c_dx': 0.3, 'c_ld': 300, 'c_lg': 0.3, 'c_lu': 0.3, 'c_lh': 0.3, 'w_ga_d1': 1, 'w_ou_g1': 1, 'o_db': 0, 'w_db_d1': 0, 'w_df_d1': 0, 'w_df_g1': 0, 'w_db_g1': 0, 'w_ua_g1': 0, 'w_ou_d2': 1, 'o_c4': 0, 'w_gb_u1': 1, 'w_gb_d2': 0, 'w_ub_u1': 0, 'o_r2u': 0, 'w_nb_d3': 1, 'w_nb_g2': 1, 'w_nb_u1': 0, 'w_ag_d3': 0, 'w_ag_g2': 0, 'o_u2': 1, 'o_g3': 1, 'o_d4': 1, 'o_u3': 0, 'o_c8': 0, 'o_dx': 0, 'w_dx_u2': 1, 'w_dx_g3': 1, 'w_dx_d4': 0, 'o_g4': 0, 'o_u4': 1, 'w_aw_g4': 0, 'w_aw_u4': 0, 'o_dx2': 0, 'o_lg': 0, 'o_lu': 0, 'w_lh': 1, 'o_ga': 1}


def on(name, values):
    return tuple(values) if PLAN[name] else ()


def cost(us=300):
    us = PLAN.get(us, us)
    return pl.CostEstimate(flops=int(us * 1e9), bytes_accessed=int(us * 3.69e6), transcendentals=0)


def anywhere(values):
    return [pl.BlockSpec(memory_space=pl.ANY)] * len(values)


def norm_project_kernel(blocks, count_in, *refs):
    parts, (gain_ref, weight_ref, normed_ref, out_ref) = refs[:count_in], refs[count_in:]

    @pl.when(pl.program_id(0) == 0)
    def _():
        gain = gain_ref[...]
        first_row = 0
        for block in blocks:
            pieces_of = []
            for i, lead in block:
                ref = parts[i]
                pieces_of.append((ref[...] if lead is None else ref[lead]).astype(F32))
            squares = sum(jnp.sum(p * p, axis=1, keepdims=True) for p in pieces_of)
            width = sum(p.shape[1] for p in pieces_of)
            inverse = lax.rsqrt(squares / width + NORM_EPS)
            column = 0
            for p in pieces_of:
                columns = pl.ds(column, p.shape[1])
                normed_ref[pl.ds(first_row, p.shape[0]), columns] = (
                    p * inverse * gain[:, column : column + p.shape[1]]
                ).astype(BF16)
                column += p.shape[1]
            first_row += pieces_of[0].shape[0]

    out_ref[...] = product(normed_ref[...], weight_ref[...], NN)


def norm_project(parts, blocks, gain, weights, columns):
    count = sum(parts[block[0][0]].shape[-2] for block in blocks)
    width = gain.shape[1]
    step = 256
    return pl.pallas_call(
        functools.partial(norm_project_kernel, blocks, len(parts)),
        out_shape=[
            jax.ShapeDtypeStruct((count, width), BF16),
            jax.ShapeDtypeStruct((count, columns), F32),
        ],
        grid=(columns // step,),
        in_specs=[resident(p.shape) for p in parts]
        + [resident((1, width)), pl.BlockSpec((width, step), lambda n: (0, n))],
        out_specs=[
            pl.BlockSpec((count, width), lambda n: (0, 0)),
            pl.BlockSpec((count, step), lambda n: (0, n)),
        ],
        compiler_params=kernel_params(),
        cost_estimate=cost('c_k0'),
    )(*parts, gain, weights)


def hidden_kernel(x_ref, cot_ref, gate_up_ref, down_ref, *refs):
    hidden_ref, both_ref, hidden_t_ref, d_gate_t_ref, d_up_t_ref = refs[-5:]
    units = down_ref.shape[0]
    gate_up = product(x_ref[...], gate_up_ref[...], NT)
    d_hidden = product(cot_ref[...], down_ref[...], NT)
    gate, up = gate_up[:, :units], gate_up[:, units:]
    sigmoid = 1.0 / (1.0 + jnp.exp(-gate))
    silu = gate * sigmoid
    hidden = (silu * up).astype(BF16)
    d_gate = (d_hidden * up * (sigmoid + silu * (1.0 - sigmoid))).astype(BF16)
    d_up = (d_hidden * silu).astype(BF16)
    hidden_ref[...] = hidden
    both_ref[:, :units] = d_gate
    both_ref[:, units:] = d_up
    hidden_t_ref[...] = hidden.T
    d_gate_t_ref[...] = d_gate.T
    d_up_t_ref[...] = d_up.T


def hidden_grads(x, cot, gate_up, down, part, before=(), waits=()):
    count, width = x.shape
    units = down.shape[0] // 2
    block = 256
    rows_in = pl.BlockSpec((block, width), lambda i: (i, 0))
    once = pl.Buffered(1)
    transposed = pl.BlockSpec((units, block), lambda i: (0, i))
    return pl.pallas_call(
        hidden_kernel,
        out_shape=[
            jax.ShapeDtypeStruct((count, 2 * units), BF16),
            jax.ShapeDtypeStruct((count, 4 * units), BF16),
        ]
        + [jax.ShapeDtypeStruct((units, count), BF16)] * 3,
        grid=(count // block,),
        in_specs=[
            rows_in,
            rows_in,
            pl.BlockSpec((2 * units, width), lambda i: (part, 0), pipeline_mode=once),
            pl.BlockSpec((units, width), lambda i: (part, 0), pipeline_mode=once),
        ]
        + anywhere((*before, *waits)),
        out_specs=[
            pl.BlockSpec((block, units), lambda i: (i, part)),
            pl.BlockSpec((block, 2 * units), lambda i: (i, part)),
        ]
        + [transposed] * 3,
        input_output_aliases={4 + i: i for i in range(len(before))},
        compiler_params=kernel_params(),
        cost_estimate=cost('c_ha' if part == 0 else 'c_hb'),
    )(x, cot, gate_up, down, *before, *waits)


def rows_product_kernel(a_ref, w_ref, *refs):
    out_ref = refs[-1]
    for rows in pieces(out_ref.shape[0], 512):
        out_ref[rows, :] = product(a_ref[rows, :], w_ref[...], NN).astype(BF16)


def rows_product(a, w, waits=(), us=300):
    count, depth = a.shape
    width = w.shape[1]
    block = 512
    return pl.pallas_call(
        rows_product_kernel,
        out_shape=jax.ShapeDtypeStruct((count, width), BF16),
        grid=(width // block,),
        in_specs=[resident((count, depth)), pl.BlockSpec((depth, block), lambda n: (0, n))]
        + anywhere(waits),
        out_specs=pl.BlockSpec((count, block), lambda n: (0, n)),
        compiler_params=kernel_params(),
        cost_estimate=cost(us),
    )(a, w, *waits)


def core_product_kernel(core_ref, a_ref, w_ref, *refs):
    kept_ref, sent_ref = refs[-2:]
    chips, height, width = kept_ref.shape
    for chip in range(chips):
        rows = pl.ds(2 * chip * height, 2 * height)
        pair = product(a_ref[rows, :], w_ref[...], NN)
        first, second = pair[:height], pair[height:]
        own_first = core_ref[0] == 0
        kept_ref[chip] = jnp.where(own_first, first, second).astype(BF16)
        sent_ref[chip] = jnp.where(own_first, second, first).astype(BF16)


def core_product(a, w, waits=(), us=300):
    count, depth = a.shape
    width = w.shape[1]
    block = 512
    chips = lax.axis_size("fsdp") // 2
    height = count // (2 * chips)
    out = pl.BlockSpec((chips, height, block), lambda n: (0, 0, n))
    return pl.pallas_call(
        core_product_kernel,
        out_shape=[jax.ShapeDtypeStruct((chips, height, width), BF16)] * 2,
        grid=(width // block,),
        in_specs=[
            pl.BlockSpec(memory_space=pltpu.SMEM),
            resident((count, depth)),
            pl.BlockSpec((depth, block), lambda n: (0, n)),
        ]
        + anywhere(waits),
        out_specs=[out, out],
        compiler_params=kernel_params(),
        cost_estimate=cost(us),
    )(own_core(), a, w, *waits)


def own_core():
    return (lax.axis_index("fsdp") % 2).astype(jnp.int32)[None]


def sum_cores(kept, sent):
    devices = lax.axis_size("fsdp")
    got = lax.ppermute(sent, "fsdp", [(i, i ^ 1) for i in range(devices)])
    return sum_low(kept, got)


def scatter_chips(x):
    devices = lax.axis_size("fsdp")
    groups = [list(range(core, devices, 2)) for core in range(2)]
    return lax.psum_scatter(
        x.reshape(-1, x.shape[-1]),
        "fsdp",
        scatter_dimension=0,
        tiled=True,
        axis_index_groups=groups,
    )


def weight_grad_kernel(a_ref, b_ref, *refs):
    first_ref, upper_ref, lower_ref = refs[-3:]
    n = pl.program_id(0)
    height = upper_ref.shape[0]
    result = product(a_ref[...], b_ref[...], NN).astype(BF16)

    @pl.when(n < 2)
    def _():
        first_ref[0] = result[:height]
        first_ref[1] = result[height:]

    @pl.when(n >= 2)
    def _():
        upper_ref[...] = result[:height]
        lower_ref[...] = result[height:]


def weight_grad(a, b, waits=(), us=300):
    units, count = a.shape
    width = b.shape[1]
    height, half, block = units // 2, width // 2, width // 4
    lone = pl.BlockSpec((height, block), lambda n: (0, jnp.maximum(n - 2, 0)))
    return pl.pallas_call(
        weight_grad_kernel,
        out_shape=[
            jax.ShapeDtypeStruct((2, height, half), BF16),
            jax.ShapeDtypeStruct((height, half), BF16),
            jax.ShapeDtypeStruct((height, half), BF16),
        ],
        grid=(4,),
        in_specs=[
            resident((units, count)),
            pl.BlockSpec((count, block), lambda n: (0, n)),
        ]
        + anywhere(waits),
        out_specs=[
            pl.BlockSpec((2, height, block), lambda n: (0, 0, jnp.minimum(n, 1))),
            lone,
            lone,
        ],
        compiler_params=kernel_params(),
        cost_estimate=cost(us),
    )(a, b, *waits)


def parts_kernel(dims, lhs_ref, rhs_ref, first_sent, first_kept, second_sent, second_kept):
    n = pl.program_id(0)
    rows = first_sent.shape[1]
    result = product(lhs_ref[...], rhs_ref[...], dims).astype(BF16)
    blocks = [result[r * rows : (r + 1) * rows] for r in range(4)]

    @pl.when(n < 2)
    def _():
        first_kept[0], first_sent[0], first_kept[1], first_sent[1] = blocks

    @pl.when(n >= 2)
    def _():
        second_kept[0], second_kept[1], second_sent[0], second_sent[1] = blocks


def product_in_parts(lhs, rhs, dims, width):
    count, depth = lhs.shape
    if not square():
        if dims == NT:
            rhs = rhs[:, :depth]
        return product(lhs, rhs, dims).astype(BF16).reshape(lax.axis_size("ctx"), -1, width)
    block = width // 4
    if dims == NT:
        rhs_spec = pl.BlockSpec((block, depth), lambda n: (n, 0))
    else:
        rhs_spec = pl.BlockSpec((depth, block), lambda n: (0, n))
    shape = (2, count // 4, width // 2)
    first = pl.BlockSpec((*shape[:2], block), lambda n: (0, 0, jnp.minimum(n, 1)))
    second = pl.BlockSpec((*shape[:2], block), lambda n: (0, 0, jnp.maximum(n - 2, 0)))
    return pl.pallas_call(
        functools.partial(parts_kernel, dims),
        out_shape=[jax.ShapeDtypeStruct(shape, BF16)] * 4,
        grid=(4,),
        in_specs=[resident((count, depth)), rhs_spec],
        out_specs=[first, first, second, second],
        compiler_params=kernel_params(),
        cost_estimate=cost('c_op' if dims == NN else 'c_dx'),
    )(lhs, rhs)


def rows_grad_kernel(terms, core_ref, *refs):
    beside_ref, kept_ref, sent_ref = refs[-3:]
    height = kept_ref.shape[1]
    own_first = core_ref[0] == 0

    def store(pair, first_column):
        columns = pl.ds(first_column, pair.shape[1])
        first, second = pair[:height], pair[height:]
        kept_ref[0, :, columns] = jnp.where(own_first, first, second).astype(BF16)
        sent_ref[0, :, columns] = jnp.where(own_first, second, first).astype(BF16)

    column = 0
    for i in range(terms):
        store(product(refs[i][...], refs[terms + i][...], TN), column)
        column += refs[terms + i].shape[1]
    store(beside_ref[...], column)


def plain_grad_kernel(terms, *refs):
    beside_ref, out_ref = refs[-2:]
    column = 0
    for i in range(terms):
        columns = pl.ds(column, refs[terms + i].shape[1])
        out_ref[:, columns] = product(refs[i][...], refs[terms + i][...], TN).astype(BF16)
        column += refs[terms + i].shape[1]
    out_ref[:, column:] = beside_ref[...].astype(BF16)


def plain_grad(terms, beside):
    count, width = terms[0][0].shape
    block = 512
    total = sum(b.shape[1] for _, b in terms) + beside.shape[1]
    return pl.pallas_call(
        functools.partial(plain_grad_kernel, len(terms)),
        out_shape=jax.ShapeDtypeStruct((width, total), BF16),
        grid=(width // block,),
        in_specs=[pl.BlockSpec((count, block), lambda m: (0, m))] * len(terms)
        + [resident(b.shape) for _, b in terms]
        + [pl.BlockSpec((block, beside.shape[1]), lambda m: (m, 0))],
        out_specs=pl.BlockSpec((block, total), lambda m: (m, 0)),
        compiler_params=kernel_params(),
        cost_estimate=cost('c_rg'),
    )(*[a for a, _ in terms], *[b for _, b in terms], beside)


def rows_grad(terms, beside):
    count, width = terms[0][0].shape
    chips = lax.axis_size("fsdp") // 2
    block = width // chips
    total = sum(b.shape[1] for _, b in terms) + beside.shape[1]
    out = pl.BlockSpec((1, block // 2, total), lambda m: (m, 0, 0))
    return pl.pallas_call(
        functools.partial(rows_grad_kernel, len(terms)),
        out_shape=[jax.ShapeDtypeStruct((chips, block // 2, total), BF16)] * 2,
        grid=(chips,),
        in_specs=[pl.BlockSpec(memory_space=pltpu.SMEM)]
        + [pl.BlockSpec((count, block), lambda m: (0, m))] * len(terms)
        + [resident(b.shape) for _, b in terms]
        + [pl.BlockSpec((block, beside.shape[1]), lambda m: (m, 0))],
        out_specs=[out, out],
        compiler_params=kernel_params(),
        cost_estimate=cost('c_rg'),
    )(own_core(), *[a for a, _ in terms], *[b for _, b in terms], beside)


def turned(x, cosine, sine):
    return x * cosine + pltpu.roll(x, HEAD_WIDTH // 2, 1) * sine


def attend_kernel(
    query_in, key_in, value_in, cos_ref, sin_ref, bias_ref, query_ref, key_ref, value_ref, probs_ref, out_ref
):
    scale = HEAD_WIDTH ** (-0.5) * LOG2_E
    key = turned(key_in[...], cos_ref[...], sin_ref[...]).astype(BF16)
    value = value_in[...].astype(BF16)
    key_ref[...] = key
    value_ref[...] = value
    for h in range(GROUP):
        head = pl.ds(h * HEAD_WIDTH, HEAD_WIDTH)
        for rows in pieces(query_in.shape[0], 256):
            query = turned(query_in[rows, head], cos_ref[rows, :], sin_ref[rows, :]).astype(BF16)
            query_ref[rows, head] = query
            scores = product(query, key, NT) * scale + bias_ref[rows, :]
            weights = jnp.exp2(scores - jnp.max(scores, axis=1, keepdims=True))
            probs = (weights * (1.0 / jnp.sum(weights, axis=1, keepdims=True))).astype(BF16)
            probs_ref[h, rows, :] = probs
            out_ref[rows, head] = product(probs, value, NN).astype(BF16)


def attend(packed, cosine, sine, bias, kv_heads):
    count = packed.shape[0]
    wide, narrow = GROUP * HEAD_WIDTH, HEAD_WIDTH
    q_heads = kv_heads * GROUP

    def column(width, first):
        return pl.BlockSpec((count, width), lambda g: (0, first + g))

    def sized(*shape):
        return jax.ShapeDtypeStruct(shape, BF16)

    return pl.pallas_call(
        attend_kernel,
        out_shape=[
            sized(count, kv_heads * wide),
            sized(count, kv_heads * narrow),
            sized(count, kv_heads * narrow),
            sized(q_heads, count, count),
            sized(count, kv_heads * wide),
        ],
        grid=(kv_heads,),
        in_specs=[
            column(wide, 0),
            column(narrow, q_heads),
            column(narrow, q_heads + kv_heads),
            resident((count, HEAD_WIDTH)),
            resident((count, HEAD_WIDTH)),
            resident((count, count)),
        ],
        out_specs=[
            column(wide, 0),
            column(narrow, 0),
            column(narrow, 0),
            pl.BlockSpec((GROUP, count, count), lambda g: (g, 0, 0)),
            column(wide, 0),
        ],
        compiler_params=kernel_params(),
        cost_estimate=cost('c_at'),
    )(packed, packed, packed, cosine, sine, bias)


def attend_back_kernel(
    blocks,
    place_ref,
    query_ref,
    key_ref,
    value_ref,
    probs_ref,
    out_ref,
    cos_ref,
    sin_ref,
    weight_ref,
    *refs,
):
    *parts, packed_ref, branch_ref, whole_ref, d_out_ref = refs
    g = pl.program_id(0)
    kv_heads = pl.num_programs(0)
    scale = HEAD_WIDTH ** (-0.5)

    @pl.when(g == 0)
    def _():
        first_row = 0
        for block in blocks:
            first = 0
            for i, lead in block:
                part = parts[i][...] if lead is None else parts[i][lead]
                height, width = part.shape
                whole_ref[pl.ds(first_row, height), pl.ds(first, width)] = part
                first += width
            first_row += height
        columns = branch_ref.shape[1]
        start = pl.multiple_of(place_ref[0] * columns, 128)
        branch_ref[...] = whole_ref[:, pl.ds(start, columns)]

    d_out_ref[...] = product(whole_ref[...], weight_ref[...], NT).astype(BF16)
    key, value = key_ref[...], value_ref[...]
    d_key = d_value = None
    for h in range(GROUP):
        head = pl.ds(h * HEAD_WIDTH, HEAD_WIDTH)
        for rows in pieces(query_ref.shape[0], 256):
            d_out = d_out_ref[rows, head]
            delta = jnp.sum(
                d_out.astype(F32) * out_ref[rows, head].astype(F32), axis=1, keepdims=True
            )
            probs = probs_ref[h, rows, :]
            d_scores = (probs.astype(F32) * (product(d_out, value, NT) - delta)).astype(BF16)
            d_query = turned(
                product(d_scores, key, NN) * scale, cos_ref[rows, :], -sin_ref[rows, :]
            )
            place = pl.multiple_of((g * GROUP + h) * HEAD_WIDTH, HEAD_WIDTH)
            packed_ref[rows, pl.ds(place, HEAD_WIDTH)] = d_query.astype(BF16)
            d_key_here = product(d_scores, query_ref[rows, head], TN)
            d_value_here = product(probs, d_out, TN)
            d_key = d_key_here if d_key is None else d_key + d_key_here
            d_value = d_value_here if d_value is None else d_value + d_value_here
    place = pl.multiple_of((kv_heads * GROUP + g) * HEAD_WIDTH, HEAD_WIDTH)
    packed_ref[:, pl.ds(place, HEAD_WIDTH)] = turned(
        d_key * scale, cos_ref[...], -sin_ref[...]
    ).astype(BF16)
    place = pl.multiple_of((kv_heads * (GROUP + 1) + g) * HEAD_WIDTH, HEAD_WIDTH)
    packed_ref[:, pl.ds(place, HEAD_WIDTH)] = d_value.astype(BF16)


def attend_back(queries, keys, values, probs, out, cosine, sine, parts, blocks, w_rows, columns):
    count = queries.shape[0]
    kv_heads = keys.shape[1] // HEAD_WIDTH
    wide, narrow = GROUP * HEAD_WIDTH, HEAD_WIDTH

    def column(width):
        return pl.BlockSpec((count, width), lambda g: (0, g))

    packed_shape = (count, kv_heads * (GROUP + 2) * HEAD_WIDTH)
    return pl.pallas_call(
        functools.partial(attend_back_kernel, blocks),
        out_shape=[
            jax.ShapeDtypeStruct(packed_shape, BF16),
            jax.ShapeDtypeStruct((count, columns), BF16),
        ],
        grid=(kv_heads,),
        in_specs=[
            pl.BlockSpec(memory_space=pltpu.SMEM),
            column(wide),
            column(narrow),
            column(narrow),
            pl.BlockSpec((GROUP, count, count), lambda g: (g, 0, 0)),
            column(wide),
            resident((count, HEAD_WIDTH)),
            resident((count, HEAD_WIDTH)),
            pl.BlockSpec((wide, w_rows.shape[1]), lambda g: (g, 0)),
        ]
        + [resident(p.shape) for p in parts],
        out_specs=[
            pl.BlockSpec(packed_shape, lambda g: (0, 0)),
            pl.BlockSpec((count, columns), lambda g: (0, 0)),
        ],
        scratch_shapes=[pltpu.VMEM((count, w_rows.shape[1]), BF16), pltpu.VMEM((count, wide), BF16)],
        compiler_params=kernel_params(),
        cost_estimate=cost('c_k4'),
    )(
        lax.axis_index("ctx").astype(jnp.int32)[None],
        queries,
        keys,
        values,
        probs,
        out,
        cosine,
        sine,
        w_rows,
        *parts,
    )


def square():
    return lax.axis_size("ctx") == 4


def swap(x, bit):
    return lax.ppermute(x, "ctx", [(i, i ^ bit) for i in range(4)])


def block_order():
    if square():
        return lax.axis_index("ctx") ^ jnp.arange(4, dtype=jnp.int32)
    return jnp.arange(lax.axis_size("ctx"), dtype=jnp.int32)


def gather_parts(x, *others):
    if not square():
        return [lax.all_gather(x, "ctx", axis=0, tiled=True)], [[(0, None)]]
    half = -(-x.shape[-1] // 256) * 128
    first, second = x[..., :half], x[..., half:]
    first_1 = swap(first, 1)
    second_2 = swap(second, 2)
    first_01, second_02 = jnp.stack([first, first_1]), jnp.stack([second, second_2])
    if others:
        first_01, second_02 = after(first_01, *others), after(second_02, *others)
    first_23 = swap(first_01, 2)
    second_13 = swap(second_02, 1)
    blocks = [[(0, None)], [(1, None), (4, 0)], [(3, 0), (2, None)], [(3, 1), (4, 1)]]
    return [x, first_1, second_2, first_23, second_13], blocks


def gather_ctx(x):
    if not square():
        return lax.all_gather(x, "ctx", axis=0)
    parts, blocks = gather_parts(x)
    return jnp.stack(
        [
            jnp.concatenate([parts[i] if lead is None else parts[i][lead] for i, lead in block], axis=-1)
            for block in blocks
        ]
    )


class ScatterSumCtx:
    def __init__(self, parts):
        self.parts = parts
        if square():
            self.got_first = swap(parts[0], 1)
            self.got_second = swap(parts[2], 2)

    def result(self, *others):
        if not square():
            return lax.psum_scatter(self.parts, "ctx", scatter_dimension=0, tiled=False).astype(F32)
        _, first_kept, _, second_kept = self.parts
        first = sum_low(first_kept[1], self.got_first[1])
        second = sum_low(second_kept[1], self.got_second[1])
        if others:
            first, second = after(first, *others), after(second, *others)
        last_first, last_second = swap(first, 2), swap(second, 1)
        return jnp.concatenate(
            [
                sum(t.astype(F32) for t in (first_kept[0], self.got_first[0], last_first)),
                sum(t.astype(F32) for t in (second_kept[0], self.got_second[0], last_second)),
            ],
            axis=-1,
        )


def absolute_order(blocks):
    if not square():
        return [blocks[i] for i in range(lax.axis_size("ctx"))]
    place = lax.axis_index("ctx")
    low, high = (place & 1) == 1, (place & 2) == 2
    a = [jnp.where(low, blocks[r ^ 1], blocks[r]) for r in range(4)]
    return [jnp.where(high, a[r ^ 2], a[r]) for r in range(4)]


def own_row_order(blocks):
    if not square():
        return blocks
    return [jnp.stack([blocks[s][r ^ s] for r in range(4)]) for s in range(4)]


def exchange_ctx(x):
    if not square():
        got = lax.all_to_all(x, "ctx", 0, 0, tiled=False)
        return [got[i] for i in range(lax.axis_size("ctx"))]
    order = block_order()
    parts = [lax.dynamic_index_in_dim(x, order[r], 0, keepdims=False) for r in range(4)]
    got = [parts[0]] + [swap(parts[r], r) for r in range(1, 4)]
    return absolute_order(got)


def nothing_kernel(*refs):
    del refs


def after(x, *others):
    if not square():
        return x
    return pl.pallas_call(
        nothing_kernel,
        out_shape=jax.ShapeDtypeStruct(x.shape, x.dtype),
        in_specs=anywhere((x, *others)),
        out_specs=anywhere((x,))[0],
        input_output_aliases={0: 0},
        cost_estimate=pl.CostEstimate(flops=0, bytes_accessed=0, transcendentals=0),
    )(x, *others)


def unit_halves(*weights):
    units = weights[0].shape[0]
    if not square():
        halves = [[w[: units // 2], w[units // 2 :]] for w in weights]
    else:
        place = lax.axis_index("ctx")
        blocks = [w.reshape(4, units // 4, w.shape[1]) for w in weights]

        def half(w, order):
            return jnp.concatenate(
                [lax.dynamic_index_in_dim(w, place ^ r, 0, keepdims=False) for r in order]
            )

        halves = [[half(w, (1, 3)), half(w, (2, 0))] for w in blocks]
    return jnp.concatenate([h[i] for i in range(2) for h in halves])


def lay_heads_kernel(blocks, sizes, place_ref, weight_ref, gain_ref, *refs):
    parts, (qkv_ref, out_ref, gain_attn_ref, gain_ffn_ref) = refs[:-4], refs[-4:]
    q_cols, kv_cols, out_cols, places = sizes
    head_cols = q_cols + 2 * kv_cols
    gain_attn = gain_ffn = 0.0
    for r, block in enumerate(blocks):
        place = place_ref[r]
        rows = jnp.concatenate(
            [parts[i][...] if lead is None else parts[i][lead] for i, lead in block], axis=1
        ).astype(F32)
        first = 0
        for width, start in (
            (q_cols, 0),
            (kv_cols, q_cols * places),
            (kv_cols, (q_cols + kv_cols) * places),
        ):
            columns = pl.ds(pl.multiple_of(start + place * width, 128), width)
            piece = rows[:, first : first + width]
            qkv_ref[:, columns] = piece
            gain_attn += jnp.sum(piece * weight_ref[:, columns].astype(F32), axis=1, keepdims=True)
            first += width
        columns = pl.ds(pl.multiple_of(place * out_cols, 128), out_cols)
        out_ref[:, columns] = rows[:, head_cols : head_cols + out_cols]
        gain_ffn += rows[:, head_cols + out_cols :]
    gain_ffn_ref[...] = gain_ffn.T[:1]
    gain_attn = jnp.broadcast_to(gain_attn, (gain_attn.shape[0], 128))
    gain_attn_ref[...] = gain_attn.T[:1] / gain_ref[...]


def lay_heads(parts, blocks, sizes, w_qkv, norm_attn, waits):
    rows, qkv_cols = w_qkv.shape
    q_cols, kv_cols, out_cols, places = sizes
    whole = pl.BlockSpec(memory_space=pltpu.VMEM)
    return pl.pallas_call(
        functools.partial(lay_heads_kernel, blocks, sizes),
        out_shape=[
            jax.ShapeDtypeStruct((rows, qkv_cols), F32),
            jax.ShapeDtypeStruct((rows, out_cols * places), F32),
            jax.ShapeDtypeStruct((1, rows), F32),
            jax.ShapeDtypeStruct((1, rows), F32),
        ],
        in_specs=[pl.BlockSpec(memory_space=pltpu.SMEM)]
        + [whole] * (2 + len(parts))
        + anywhere(waits),
        out_specs=[whole] * 4,
        compiler_params=kernel_params(),
        cost_estimate=cost('c_lh'),
    )(block_order(), w_qkv, norm_attn.astype(F32)[None, :], *parts, *waits)


def lay_out_kernel(place_ref, first_own, first_got, second_own, second_got, *refs):
    out_ref = refs[-1]
    step = pl.program_id(0)
    for i, block in enumerate((first_own, first_got, second_own, second_got)):

        @pl.when(step // 2 == i)
        def _(block=block):
            out_ref[...] = block[0].astype(F32)


def lay_out(first_own, first_got, second_own, second_got, waits, us):
    _, height, half = first_own.shape
    places = lax.axis_index("ctx") ^ jnp.array([0, 2, 1, 3, 0, 1, 2, 3], jnp.int32)

    def block_of(i):
        return pl.BlockSpec(
            (1, height, half), lambda g, where: (jnp.clip(g - 2 * i, 0, 1), 0, 0)
        )

    return pl.pallas_call(
        lay_out_kernel,
        out_shape=jax.ShapeDtypeStruct((4 * height, 2 * half), F32),
        grid_spec=pltpu.PrefetchScalarGridSpec(
            num_scalar_prefetch=1,
            grid=(8,),
            in_specs=[block_of(i) for i in range(4)] + anywhere(waits),
            out_specs=pl.BlockSpec((height, half), lambda g, where: (where[g], g // 4)),
        ),
        compiler_params=pltpu.CompilerParams(vmem_limit_bytes=32 * 2**20),
        cost_estimate=cost(us),
    )(places, first_own, first_got, second_own, second_got, *waits)


def sum_low(*terms):
    return sum(t.astype(F32) for t in terms).astype(BF16)


class SumCtx:
    def start_first(self, part):
        self.upper = part
        if not square():
            return
        self.got_first = swap(part[0], 1)
        self.got_third = swap(part[2], 2)

    def start_second(self, part, *others):
        self.lower = part
        if not square():
            blocks = []
            for first, upper, lower in (self.upper, part):
                second = jnp.stack([upper, lower])
                blocks.append(jnp.concatenate([first, second], axis=-1))
            whole = jnp.concatenate(blocks)
            self.whole = lax.psum(whole.reshape(-1, whole.shape[-1]), "ctx").astype(F32)
            return
        self.got_second = swap(after(part[1], *others) if others else part[1], 2)

    def arrived(self, second=False):
        if not square():
            return ()
        return (self.got_second,) if second else (self.got_first, self.got_third)

    def step_2(self, *others):
        if not square():
            return ()
        first = sum_low(self.lower[0][0], self.got_first[1])
        second = sum_low(self.upper[1], self.got_third)
        self.last_first = swap(after(first, *others) if others else first, 2)
        self.last_second = swap(after(second, *others) if others else second, 1)
        return (self.last_first, self.last_second)

    def step_3(self, *others):
        if not square():
            return ()
        self.first = sum_low(self.lower[0][1], self.got_first[0], self.last_first)
        self.second = sum_low(self.lower[2], self.got_second, self.last_second)
        if others:
            self.first = after(self.first, *others)
            self.second = after(self.second, *others)
        self.first_2 = swap(self.first, 2)
        self.second_1 = swap(self.second, 1)
        return (self.first_2, self.second_1)

    def step_4(self, *others):
        if not square():
            return ()
        self.first_02 = jnp.stack([self.first, self.first_2])
        self.second_01 = jnp.stack([self.second, self.second_1])
        if others:
            self.first_02 = after(self.first_02, *others)
            self.second_01 = after(self.second_01, *others)
        self.first_13 = swap(self.first_02, 1)
        self.second_23 = swap(self.second_01, 2)
        return (self.first_13, self.second_23)

    def result(self, waits=(), us=300):
        if not square():
            return self.whole
        return lay_out(self.first_02, self.first_13, self.second_01, self.second_23, waits, us)


def local(
    tokens,
    cotangent,
    norm_attn,
    w_qkv,
    w_out,
    norm_ffn,
    w_gate,
    w_up,
    w_down,
    seq_len,
    window,
    global_pos,
):
    places = lax.axis_size("ctx")
    place = lax.axis_index("ctx")
    shards = lax.axis_size("fsdp")
    rows = tokens.shape[1]
    width = tokens.shape[2]
    count = places * rows
    kv_heads = KEY_VALUE_HEADS // places
    q_heads = kv_heads * GROUP
    q_cols = q_heads * HEAD_WIDTH
    kv_cols = kv_heads * HEAD_WIDTH
    q_all = QUERY_HEADS * HEAD_WIDTH
    kv_all = KEY_VALUE_HEADS * HEAD_WIDTH
    out_cols = width // places
    length = seq_len[0]
    window_now = window[0]
    global_here = global_pos[0]
    x_own = tokens[0]
    cot_own = cotangent[0]

    head_cols = q_cols + 2 * kv_cols
    weights_mine = jnp.concatenate(
        [
            lax.dynamic_slice_in_dim(w_qkv, place * q_cols, q_cols, 1),
            lax.dynamic_slice_in_dim(w_qkv, q_all + place * kv_cols, kv_cols, 1),
            lax.dynamic_slice_in_dim(w_qkv, q_all + kv_all + place * kv_cols, kv_cols, 1),
            lax.dynamic_slice_in_dim(w_out, place * out_cols, out_cols, 1),
        ],
        axis=1,
    )
    weights = lax.all_gather(weights_mine, "fsdp", axis=0, tiled=True)
    gains = lax.all_gather(jnp.stack([norm_attn, norm_ffn]), "fsdp", axis=1, tiled=True)
    gain_attn = gains[0].astype(F32)
    gain_ffn = gains[1].astype(F32)
    x_parts, x_blocks = gather_parts(x_own, gains)
    cot_all = lax.all_gather(after(cot_own, *x_parts[-2:]), "fsdp", axis=0, tiled=True)
    gate_up = unit_halves(w_gate, w_up)
    down = unit_halves(w_down)
    w_rows = jnp.concatenate(
        exchange_ctx(weights[:, head_cols:].reshape(places, q_cols, out_cols)), axis=1
    )

    normed_low, packed = norm_project(x_parts, x_blocks, gain_attn[None, :], weights, head_cols)
    order = block_order()
    positions = (order[:, None] * rows + jnp.arange(rows, dtype=jnp.int32)[None, :]).reshape(count)
    cosine, sine = rope_tables(positions)
    is_global = jnp.any(positions[:, None] == global_here[None, :], axis=1)
    allowed = (
        (positions[None, :] <= positions[:, None])
        & (positions[None, :] < length)
        & (
            (positions[:, None] - positions[None, :] < window_now)
            | is_global[:, None]
            | is_global[None, :]
        )
    )
    bias = jnp.where(allowed, 0.0, NEGATIVE_FILLER)
    queries, keys, values, probs, attended_low = attend(packed, cosine, sine, bias, kv_heads)
    branch = ScatterSumCtx(product_in_parts(attended_low, w_rows, NN, width)).result()

    x_full = x_own.astype(F32)
    middle = x_full + branch
    inv_ffn = lax.rsqrt(jnp.mean(middle * middle, axis=-1, keepdims=True) + NORM_EPS)
    normed_ffn = middle * inv_ffn
    ffn_low = (normed_ffn * gain_ffn[None, :]).astype(BF16)
    ffn_all = lax.all_gather(after(ffn_low, cot_all), "fsdp", axis=0, tiled=True)
    attended_all = jnp.concatenate(
        absolute_order(own_row_order(gather_ctx(attended_low.reshape(places, rows, q_cols)))), axis=-1
    ).reshape(count, q_all)
    sum_down, sum_gate, sum_up = SumCtx(), SumCtx(), SumCtx()
    hidden, d_both, *first_t = hidden_grads(ffn_all, cot_all, gate_up, down, 0, (), (attended_all,))
    down_a = weight_grad(first_t[0], cot_all, (), "c_da")
    sum_down.start_first(down_a)
    hidden, d_both, *second_t = hidden_grads(
        ffn_all, cot_all, gate_up, down, 1, (hidden, d_both), down_a
    )
    last = (second_t[0],)
    if PLAN["o_ga"] == 0:
        gate_a = weight_grad(
            first_t[1], ffn_all, (*last, *on("w_ga_d1", sum_down.arrived())), "c_ga"
        )
        sum_gate.start_first(gate_a)
        last = gate_a
    if PLAN["o_db"]:
        down_b = weight_grad(
            second_t[0], cot_all, (*last, *on("w_db_d1", sum_down.arrived())), "c_db"
        )
        last = down_b
    d_ffn_part = rows_product(
        d_both,
        gate_up,
        (
            *last,
            *on("w_df_d1", sum_down.arrived()),
            *(on("w_df_g1", sum_gate.arrived()) if PLAN["o_ga"] == 0 else ()),
        ),
        "c_df",
    )
    d_ffn = lax.psum_scatter(d_ffn_part, "fsdp", scatter_dimension=0, tiled=True)
    last = (d_ffn_part,)
    if PLAN["o_ga"] == 1:
        gate_a = weight_grad(
            first_t[1], ffn_all, (*last, *on("w_ga_d1", sum_down.arrived())), "c_ga"
        )
        sum_gate.start_first(gate_a)
        last = gate_a
    if not PLAN["o_db"]:
        down_b = weight_grad(
            second_t[0], cot_all, (*last, *(on("w_db_g1", sum_gate.arrived()) if PLAN["o_ga"] < 2 else ())), "c_db"
        )
        last = down_b
    sum_down.start_second(down_b)
    down_2 = sum_down.step_2()
    if PLAN["o_ga"] == 2:
        gate_a = weight_grad(
            first_t[1], ffn_all, (*last, *on("w_ga_d1", sum_down.arrived())), "c_ga"
        )
        sum_gate.start_first(gate_a)
        last = gate_a
    up_a = weight_grad(first_t[2], ffn_all, (*last, *on("w_ua_g1", sum_gate.arrived())), "c_ua")
    sum_up.start_first(up_a)
    waits = (
        *up_a,
        *on("w_ou_d2", (*down_2, *sum_down.arrived(True))),
        *on("w_ou_g1", sum_gate.arrived()),
    )
    if PLAN["o_c4"]:
        ffn_part = sum_cores(*core_product(hidden, down, waits, "c_ou"))
    else:
        ffn_part = rows_product(hidden, down, waits, "c_ou")
    gate_b = weight_grad(
        second_t[1],
        ffn_all,
        (
            ffn_part,
            *on("w_gb_u1", sum_up.arrived()),
            *on("w_gb_d2", (*down_2, *sum_down.arrived(True))),
        ),
        "c_gb",
    )
    sum_gate.start_second(gate_b)
    gate_2 = sum_gate.step_2()
    down_3 = sum_down.step_3()
    up_b = weight_grad(
        second_t[2], ffn_all, (*gate_b, *on("w_ub_u1", sum_up.arrived())), "c_ub"
    )
    if not PLAN["o_r2u"]:
        sum_up.start_second(up_b)
    d_ffn = after(
        d_ffn,
        *up_b,
        *on("w_nb_d3", down_3),
        *on("w_nb_g2", gate_2),
        *on("w_nb_u1", sum_up.arrived()),
    )
    if PLAN["o_c4"]:
        ffn_sum = scatter_chips(ffn_part)
    else:
        ffn_sum = lax.psum_scatter(ffn_part, "fsdp", scatter_dimension=0, tiled=True)
    layer_out = middle + ffn_sum.astype(F32)

    d_ffn = d_ffn.astype(F32)
    scaled = d_ffn * gain_ffn[None, :]
    d_gain_ffn = jnp.sum(d_ffn * normed_ffn, axis=0)
    d_middle = cot_own.astype(F32) + inv_ffn * (
        scaled - normed_ffn * jnp.mean(scaled * normed_ffn, axis=-1, keepdims=True)
    )
    d_branch_own = d_middle.astype(BF16)
    branch_parts, branch_blocks = gather_parts(
        d_branch_own, *on("w_ag_d3", down_3), *on("w_ag_g2", gate_2)
    )
    arrived = branch_parts[-2:]
    if PLAN["o_r2u"]:
        sum_up.start_second(up_b, *arrived)
    up_2 = sum_up.step_2(*on("o_u2", arrived))
    gate_3 = sum_gate.step_3(*on("o_g3", arrived))
    down_4 = sum_down.step_4(*on("o_d4", arrived))
    d_packed, branch_cols = attend_back(
        queries,
        keys,
        values,
        probs,
        attended_low,
        cosine,
        sine,
        branch_parts,
        branch_blocks,
        w_rows,
        out_cols,
    )
    up_3 = sum_up.step_3(*on("o_u3", (d_packed,)))
    gain_cols = jnp.broadcast_to(d_gain_ffn[:, None], (width, 128))
    terms = [(normed_low, d_packed), (attended_all, branch_cols)]
    if PLAN["o_c8"]:
        by_core = rows_grad(terms, gain_cols)
        d_weights = sum_cores(*by_core)
    else:
        by_core = [plain_grad(terms, gain_cols)]
        d_weights = by_core[0]
    d_weights = after(d_weights, ffn_sum)
    d_attn_parts = product_in_parts(
        after(
            d_packed,
            d_weights if PLAN["o_dx"] else by_core[0],
            *on("w_dx_u2", up_2),
            *on("w_dx_g3", gate_3),
            *on("w_dx_d4", down_4),
        ),
        weights,
        NT,
        width,
    )
    if PLAN["o_c8"]:
        scattered = scatter_chips(d_weights)
    else:
        scattered = lax.psum_scatter(d_weights, "fsdp", scatter_dimension=0, tiled=True)
    d_attn_sum = ScatterSumCtx(d_attn_parts)
    gate_4 = sum_gate.step_4(*on("o_g4", (d_weights,)))
    up_4 = sum_up.step_4(*on("o_u4", (d_weights,)))
    grad_down = sum_down.result(d_attn_parts, "c_ld")
    parts, blocks = gather_parts(
        after(scattered, grad_down, *on("w_aw_g4", gate_4), *on("w_aw_u4", up_4))
    )
    if not square():
        rows_here = scattered.shape[0]
        parts = [parts[0].reshape(places, rows_here, -1)]
        blocks = [[(0, i)] for i in range(places)]
    d_attn = d_attn_sum.result(*on("o_dx2", parts[1:3]))
    inv_own = lax.rsqrt(jnp.mean(x_full * x_full, axis=-1, keepdims=True) + NORM_EPS)
    normed_attn = x_full * inv_own
    scaled_attn = d_attn * gain_attn[None, :]
    d_tokens = d_middle + inv_own * (
        scaled_attn - normed_attn * jnp.mean(scaled_attn * normed_attn, axis=-1, keepdims=True)
    )
    grad_gate = sum_gate.result(on("o_lg", parts[1:3]), "c_lg")
    grad_up = sum_up.result(on("o_lu", parts[1:3]), "c_lu")
    grad_qkv, grad_out, grad_gain_attn, grad_gain_ffn = lay_heads(
        parts,
        blocks,
        (q_cols, kv_cols, out_cols, places),
        w_qkv,
        norm_attn,
        on("w_lh", (grad_up,)),
    )
    return (
        layer_out.astype(BF16)[None],
        d_tokens[None],
        grad_gain_attn[0],
        grad_qkv,
        grad_out,
        grad_gain_ffn[0],
        grad_gate,
        grad_up,
        grad_down,
    )


def solution(mesh):
    return jax.shard_map(
        local,
        mesh=mesh,
        in_specs=(
            P("fsdp", "ctx", None),
            P("fsdp", "ctx", None),
            P("fsdp"),
            P("fsdp", None),
            P("fsdp", None),
            P("fsdp"),
            P("fsdp", None),
            P("fsdp", None),
            P("fsdp", None),
            P("fsdp"),
            P("fsdp"),
            P("fsdp", None),
        ),
        out_specs=(
            P("fsdp", "ctx", None),
            P("fsdp", "ctx", None),
            P("fsdp"),
            P("fsdp", None),
            P("fsdp", None),
            P("fsdp"),
            P("fsdp", None),
            P("fsdp", None),
            P("fsdp", None),
        ),
        check_vma=False,
    )
```

```python
import functools

import jax
import jax.numpy as jnp
from jax import lax
from jax.experimental import pallas as pl
from jax.experimental.pallas import tpu as pltpu
from jax.sharding import PartitionSpec as P

QUERY_HEADS = 16
KEY_VALUE_HEADS = 8
HEAD_WIDTH = 128
GROUP = QUERY_HEADS // KEY_VALUE_HEADS

NORM_EPS = 1e-05
NEGATIVE_FILLER = -1e30
ROPE_BASE = 1000000.0
LOG2_E = 1.4426950408889634
BF16 = jnp.bfloat16
F32 = jnp.float32


def rope_tables(positions):
    half_width = HEAD_WIDTH // 2
    frequency = ROPE_BASE ** (-(2.0 * jnp.arange(half_width, dtype=F32)) / HEAD_WIDTH)
    angle_table = positions.astype(F32)[:, None] * frequency[None, :]
    cosine, sine = jnp.cos(angle_table), jnp.sin(angle_table)
    return (
        jnp.concatenate([cosine, cosine], axis=1),
        jnp.concatenate([-sine, sine], axis=1),
    )


NT = (((1,), (1,)), ((), ()))
NN = (((1,), (0,)), ((), ()))
TN = (((0,), (0,)), ((), ()))
VMEM_LIMIT = 56 * 2**20


def product(a, b, dims):
    return lax.dot_general(a, b, dims, preferred_element_type=F32)


def pieces(length, most):
    size = most if length % most == 0 else length
    return [pl.ds(start, size) for start in range(0, length, size)]


def resident(shape):
    return pl.BlockSpec(shape, lambda i: (0,) * len(shape), pipeline_mode=pl.Buffered(1))


def kernel_params():
    return pltpu.CompilerParams(vmem_limit_bytes=VMEM_LIMIT)


PLAN = {'c_k0': 0.3, 'c_ha': 0.3, 'c_da': 0.3, 'c_hb': 0.3, 'c_ga': 0.3, 'c_df': 0.3, 'c_db': 0.3, 'c_ua': 300, 'c_ou': 300, 'c_gb': 300, 'c_ub': 300, 'c_op': 0.3, 'c_at': 0.3, 'c_k4': 0.3, 'c_rg': 0.3, 'c_dx': 0.3, 'c_ld': 300, 'c_lg': 0.3, 'c_lu': 0.3, 'c_lh': 0.3, 'w_ga_d1': 1, 'w_ou_g1': 1, 'o_db': 0, 'w_db_d1': 0, 'w_df_d1': 0, 'w_df_g1': 0, 'w_db_g1': 0, 'w_ua_g1': 0, 'w_ou_d2': 1, 'o_c4': 0, 'w_gb_u1': 1, 'w_gb_d2': 0, 'w_ub_u1': 0, 'o_r2u': 0, 'w_nb_d3': 1, 'w_nb_g2': 1, 'w_nb_u1': 0, 'w_ag_d3': 0, 'w_ag_g2': 0, 'o_u2': 1, 'o_g3': 1, 'o_d4': 1, 'o_u3': 0, 'o_c8': 0, 'o_dx': 0, 'w_dx_u2': 1, 'w_dx_g3': 1, 'w_dx_d4': 0, 'o_g4': 0, 'o_u4': 1, 'w_aw_g4': 0, 'w_aw_u4': 0, 'o_dx2': 0, 'o_lg': 0, 'o_lu': 0, 'w_lh': 1, 'o_ga': 1}


def on(name, values):
    return tuple(values) if PLAN[name] else ()


def cost(us=300):
    us = PLAN.get(us, us)
    return pl.CostEstimate(flops=int(us * 1e9), bytes_accessed=int(us * 3.69e6), transcendentals=0)


def anywhere(values):
    return [pl.BlockSpec(memory_space=pl.ANY)] * len(values)


def norm_project_kernel(blocks, count_in, *refs):
    parts, (gain_ref, weight_ref, normed_ref, out_ref) = refs[:count_in], refs[count_in:]

    @pl.when(pl.program_id(0) == 0)
    def _():
        gain = gain_ref[...]
        first_row = 0
        for block in blocks:
            pieces_of = []
            for i, lead in block:
                ref = parts[i]
                pieces_of.append((ref[...] if lead is None else ref[lead]).astype(F32))
            squares = sum(jnp.sum(p * p, axis=1, keepdims=True) for p in pieces_of)
            width = sum(p.shape[1] for p in pieces_of)
            inverse = lax.rsqrt(squares / width + NORM_EPS)
            column = 0
            for p in pieces_of:
                columns = pl.ds(column, p.shape[1])
                normed_ref[pl.ds(first_row, p.shape[0]), columns] = (
                    p * inverse * gain[:, column : column + p.shape[1]]
                ).astype(BF16)
                column += p.shape[1]
            first_row += pieces_of[0].shape[0]

    out_ref[...] = product(normed_ref[...], weight_ref[...], NN)


def norm_project(parts, blocks, gain, weights, columns):
    count = sum(parts[block[0][0]].shape[-2] for block in blocks)
    width = gain.shape[1]
    step = 256
    return pl.pallas_call(
        functools.partial(norm_project_kernel, blocks, len(parts)),
        out_shape=[
            jax.ShapeDtypeStruct((count, width), BF16),
            jax.ShapeDtypeStruct((count, columns), F32),
        ],
        grid=(columns // step,),
        in_specs=[resident(p.shape) for p in parts]
        + [resident((1, width)), pl.BlockSpec((width, step), lambda n: (0, n))],
        out_specs=[
            pl.BlockSpec((count, width), lambda n: (0, 0)),
            pl.BlockSpec((count, step), lambda n: (0, n)),
        ],
        compiler_params=kernel_params(),
        cost_estimate=cost('c_k0'),
    )(*parts, gain, weights)


def hidden_kernel(x_ref, cot_ref, gate_up_ref, down_ref, *refs):
    hidden_ref, both_ref, hidden_t_ref, d_gate_t_ref, d_up_t_ref = refs[-5:]
    units = down_ref.shape[0]
    gate_up = product(x_ref[...], gate_up_ref[...], NT)
    d_hidden = product(cot_ref[...], down_ref[...], NT)
    gate, up = gate_up[:, :units], gate_up[:, units:]
    sigmoid = 1.0 / (1.0 + jnp.exp(-gate))
    silu = gate * sigmoid
    hidden = (silu * up).astype(BF16)
    d_gate = (d_hidden * up * (sigmoid + silu * (1.0 - sigmoid))).astype(BF16)
    d_up = (d_hidden * silu).astype(BF16)
    hidden_ref[...] = hidden
    both_ref[:, :units] = d_gate
    both_ref[:, units:] = d_up
    hidden_t_ref[...] = hidden.T
    d_gate_t_ref[...] = d_gate.T
    d_up_t_ref[...] = d_up.T


def hidden_grads(x, cot, gate_up, down, part, before=(), waits=()):
    count, width = x.shape
    units = down.shape[0] // 2
    block = 256
    rows_in = pl.BlockSpec((block, width), lambda i: (i, 0))
    once = pl.Buffered(1)
    transposed = pl.BlockSpec((units, block), lambda i: (0, i))
    return pl.pallas_call(
        hidden_kernel,
        out_shape=[
            jax.ShapeDtypeStruct((count, 2 * units), BF16),
            jax.ShapeDtypeStruct((count, 4 * units), BF16),
        ]
        + [jax.ShapeDtypeStruct((units, count), BF16)] * 3,
        grid=(count // block,),
        in_specs=[
            rows_in,
            rows_in,
            pl.BlockSpec((2 * units, width), lambda i: (part, 0), pipeline_mode=once),
            pl.BlockSpec((units, width), lambda i: (part, 0), pipeline_mode=once),
        ]
        + anywhere((*before, *waits)),
        out_specs=[
            pl.BlockSpec((block, units), lambda i: (i, part)),
            pl.BlockSpec((block, 2 * units), lambda i: (i, part)),
        ]
        + [transposed] * 3,
        input_output_aliases={4 + i: i for i in range(len(before))},
        compiler_params=kernel_params(),
        cost_estimate=cost('c_ha' if part == 0 else 'c_hb'),
    )(x, cot, gate_up, down, *before, *waits)


def rows_product_kernel(a_ref, w_ref, *refs):
    out_ref = refs[-1]
    for rows in pieces(out_ref.shape[0], 512):
        out_ref[rows, :] = product(a_ref[rows, :], w_ref[...], NN).astype(BF16)


def rows_product(a, w, waits=(), us=300):
    count, depth = a.shape
    width = w.shape[1]
    block = 512
    return pl.pallas_call(
        rows_product_kernel,
        out_shape=jax.ShapeDtypeStruct((count, width), BF16),
        grid=(width // block,),
        in_specs=[resident((count, depth)), pl.BlockSpec((depth, block), lambda n: (0, n))]
        + anywhere(waits),
        out_specs=pl.BlockSpec((count, block), lambda n: (0, n)),
        compiler_params=kernel_params(),
        cost_estimate=cost(us),
    )(a, w, *waits)


def core_product_kernel(core_ref, a_ref, w_ref, *refs):
    kept_ref, sent_ref = refs[-2:]
    chips, height, width = kept_ref.shape
    for chip in range(chips):
        rows = pl.ds(2 * chip * height, 2 * height)
        pair = product(a_ref[rows, :], w_ref[...], NN)
        first, second = pair[:height], pair[height:]
        own_first = core_ref[0] == 0
        kept_ref[chip] = jnp.where(own_first, first, second).astype(BF16)
        sent_ref[chip] = jnp.where(own_first, second, first).astype(BF16)


def core_product(a, w, waits=(), us=300):
    count, depth = a.shape
    width = w.shape[1]
    block = 512
    chips = lax.axis_size("fsdp") // 2
    height = count // (2 * chips)
    out = pl.BlockSpec((chips, height, block), lambda n: (0, 0, n))
    return pl.pallas_call(
        core_product_kernel,
        out_shape=[jax.ShapeDtypeStruct((chips, height, width), BF16)] * 2,
        grid=(width // block,),
        in_specs=[
            pl.BlockSpec(memory_space=pltpu.SMEM),
            resident((count, depth)),
            pl.BlockSpec((depth, block), lambda n: (0, n)),
        ]
        + anywhere(waits),
        out_specs=[out, out],
        compiler_params=kernel_params(),
        cost_estimate=cost(us),
    )(own_core(), a, w, *waits)


def own_core():
    return (lax.axis_index("fsdp") % 2).astype(jnp.int32)[None]


def sum_cores(kept, sent):
    devices = lax.axis_size("fsdp")
    got = lax.ppermute(sent, "fsdp", [(i, i ^ 1) for i in range(devices)])
    return sum_low(kept, got)


def scatter_chips(x):
    devices = lax.axis_size("fsdp")
    groups = [list(range(core, devices, 2)) for core in range(2)]
    return lax.psum_scatter(
        x.reshape(-1, x.shape[-1]),
        "fsdp",
        scatter_dimension=0,
        tiled=True,
        axis_index_groups=groups,
    )


def weight_grad_kernel(a_ref, b_ref, *refs):
    first_ref, upper_ref, lower_ref = refs[-3:]
    n = pl.program_id(0)
    height = upper_ref.shape[0]
    result = product(a_ref[...], b_ref[...], NN).astype(BF16)

    @pl.when(n < 2)
    def _():
        first_ref[0] = result[:height]
        first_ref[1] = result[height:]

    @pl.when(n >= 2)
    def _():
        upper_ref[...] = result[:height]
        lower_ref[...] = result[height:]


def weight_grad(a, b, waits=(), us=300):
    units, count = a.shape
    width = b.shape[1]
    height, half, block = units // 2, width // 2, width // 4
    lone = pl.BlockSpec((height, block), lambda n: (0, jnp.maximum(n - 2, 0)))
    return pl.pallas_call(
        weight_grad_kernel,
        out_shape=[
            jax.ShapeDtypeStruct((2, height, half), BF16),
            jax.ShapeDtypeStruct((height, half), BF16),
            jax.ShapeDtypeStruct((height, half), BF16),
        ],
        grid=(4,),
        in_specs=[
            resident((units, count)),
            pl.BlockSpec((count, block), lambda n: (0, n)),
        ]
        + anywhere(waits),
        out_specs=[
            pl.BlockSpec((2, height, block), lambda n: (0, 0, jnp.minimum(n, 1))),
            lone,
            lone,
        ],
        compiler_params=kernel_params(),
        cost_estimate=cost(us),
    )(a, b, *waits)


def parts_kernel(dims, lhs_ref, rhs_ref, first_sent, first_kept, second_sent, second_kept):
    n = pl.program_id(0)
    rows = first_sent.shape[1]
    result = product(lhs_ref[...], rhs_ref[...], dims).astype(BF16)
    blocks = [result[r * rows : (r + 1) * rows] for r in range(4)]

    @pl.when(n < 2)
    def _():
        first_kept[0], first_sent[0], first_kept[1], first_sent[1] = blocks

    @pl.when(n >= 2)
    def _():
        second_kept[0], second_kept[1], second_sent[0], second_sent[1] = blocks


def product_in_parts(lhs, rhs, dims, width):
    count, depth = lhs.shape
    if not square():
        if dims == NT:
            rhs = rhs[:, :depth]
        return product(lhs, rhs, dims).astype(BF16).reshape(lax.axis_size("ctx"), -1, width)
    block = width // 4
    if dims == NT:
        rhs_spec = pl.BlockSpec((block, depth), lambda n: (n, 0))
    else:
        rhs_spec = pl.BlockSpec((depth, block), lambda n: (0, n))
    shape = (2, count // 4, width // 2)
    first = pl.BlockSpec((*shape[:2], block), lambda n: (0, 0, jnp.minimum(n, 1)))
    second = pl.BlockSpec((*shape[:2], block), lambda n: (0, 0, jnp.maximum(n - 2, 0)))
    return pl.pallas_call(
        functools.partial(parts_kernel, dims),
        out_shape=[jax.ShapeDtypeStruct(shape, BF16)] * 4,
        grid=(4,),
        in_specs=[resident((count, depth)), rhs_spec],
        out_specs=[first, first, second, second],
        compiler_params=kernel_params(),
        cost_estimate=cost('c_op' if dims == NN else 'c_dx'),
    )(lhs, rhs)


def rows_grad_kernel(terms, core_ref, *refs):
    beside_ref, kept_ref, sent_ref = refs[-3:]
    height = kept_ref.shape[1]
    own_first = core_ref[0] == 0

    def store(pair, first_column):
        columns = pl.ds(first_column, pair.shape[1])
        first, second = pair[:height], pair[height:]
        kept_ref[0, :, columns] = jnp.where(own_first, first, second).astype(BF16)
        sent_ref[0, :, columns] = jnp.where(own_first, second, first).astype(BF16)

    column = 0
    for i in range(terms):
        store(product(refs[i][...], refs[terms + i][...], TN), column)
        column += refs[terms + i].shape[1]
    store(beside_ref[...], column)


def plain_grad_kernel(terms, *refs):
    beside_ref, out_ref = refs[-2:]
    column = 0
    for i in range(terms):
        columns = pl.ds(column, refs[terms + i].shape[1])
        out_ref[:, columns] = product(refs[i][...], refs[terms + i][...], TN).astype(BF16)
        column += refs[terms + i].shape[1]
    out_ref[:, column:] = beside_ref[...].astype(BF16)


def plain_grad(terms, beside):
    count, width = terms[0][0].shape
    block = 512
    total = sum(b.shape[1] for _, b in terms) + beside.shape[1]
    return pl.pallas_call(
        functools.partial(plain_grad_kernel, len(terms)),
        out_shape=jax.ShapeDtypeStruct((width, total), BF16),
        grid=(width // block,),
        in_specs=[pl.BlockSpec((count, block), lambda m: (0, m))] * len(terms)
        + [resident(b.shape) for _, b in terms]
        + [pl.BlockSpec((block, beside.shape[1]), lambda m: (m, 0))],
        out_specs=pl.BlockSpec((block, total), lambda m: (m, 0)),
        compiler_params=kernel_params(),
        cost_estimate=cost('c_rg'),
    )(*[a for a, _ in terms], *[b for _, b in terms], beside)


def rows_grad(terms, beside):
    count, width = terms[0][0].shape
    chips = lax.axis_size("fsdp") // 2
    block = width // chips
    total = sum(b.shape[1] for _, b in terms) + beside.shape[1]
    out = pl.BlockSpec((1, block // 2, total), lambda m: (m, 0, 0))
    return pl.pallas_call(
        functools.partial(rows_grad_kernel, len(terms)),
        out_shape=[jax.ShapeDtypeStruct((chips, block // 2, total), BF16)] * 2,
        grid=(chips,),
        in_specs=[pl.BlockSpec(memory_space=pltpu.SMEM)]
        + [pl.BlockSpec((count, block), lambda m: (0, m))] * len(terms)
        + [resident(b.shape) for _, b in terms]
        + [pl.BlockSpec((block, beside.shape[1]), lambda m: (m, 0))],
        out_specs=[out, out],
        compiler_params=kernel_params(),
        cost_estimate=cost('c_rg'),
    )(own_core(), *[a for a, _ in terms], *[b for _, b in terms], beside)


def turned(x, cosine, sine):
    return x * cosine + pltpu.roll(x, HEAD_WIDTH // 2, 1) * sine


def attend_kernel(
    query_in, key_in, value_in, cos_ref, sin_ref, bias_ref, query_ref, key_ref, value_ref, probs_ref, out_ref
):
    scale = HEAD_WIDTH ** (-0.5) * LOG2_E
    key = turned(key_in[...], cos_ref[...], sin_ref[...]).astype(BF16)
    value = value_in[...].astype(BF16)
    key_ref[...] = key
    value_ref[...] = value
    for h in range(GROUP):
        head = pl.ds(h * HEAD_WIDTH, HEAD_WIDTH)
        for rows in pieces(query_in.shape[0], 384):
            query = turned(query_in[rows, head], cos_ref[rows, :], sin_ref[rows, :]).astype(BF16)
            query_ref[rows, head] = query
            scores = product(query, key, NT) * scale + bias_ref[rows, :]
            weights = jnp.exp2(scores - jnp.max(scores, axis=1, keepdims=True))
            probs = (weights * (1.0 / jnp.sum(weights, axis=1, keepdims=True))).astype(BF16)
            probs_ref[h, rows, :] = probs
            out_ref[rows, head] = product(probs, value, NN).astype(BF16)


def attend(packed, cosine, sine, bias, kv_heads):
    count = packed.shape[0]
    wide, narrow = GROUP * HEAD_WIDTH, HEAD_WIDTH
    q_heads = kv_heads * GROUP

    def column(width, first):
        return pl.BlockSpec((count, width), lambda g: (0, first + g))

    def sized(*shape):
        return jax.ShapeDtypeStruct(shape, BF16)

    return pl.pallas_call(
        attend_kernel,
        out_shape=[
            sized(count, kv_heads * wide),
            sized(count, kv_heads * narrow),
            sized(count, kv_heads * narrow),
            sized(q_heads, count, count),
            sized(count, kv_heads * wide),
        ],
        grid=(kv_heads,),
        in_specs=[
            column(wide, 0),
            column(narrow, q_heads),
            column(narrow, q_heads + kv_heads),
            resident((count, HEAD_WIDTH)),
            resident((count, HEAD_WIDTH)),
            resident((count, count)),
        ],
        out_specs=[
            column(wide, 0),
            column(narrow, 0),
            column(narrow, 0),
            pl.BlockSpec((GROUP, count, count), lambda g: (g, 0, 0)),
            column(wide, 0),
        ],
        compiler_params=kernel_params(),
        cost_estimate=cost('c_at'),
    )(packed, packed, packed, cosine, sine, bias)


def attend_back_kernel(
    blocks,
    place_ref,
    query_ref,
    key_ref,
    value_ref,
    probs_ref,
    out_ref,
    cos_ref,
    sin_ref,
    weight_ref,
    *refs,
):
    *parts, packed_ref, branch_ref, whole_ref, d_out_ref = refs
    g = pl.program_id(0)
    kv_heads = pl.num_programs(0)
    scale = HEAD_WIDTH ** (-0.5)

    @pl.when(g == 0)
    def _():
        first_row = 0
        for block in blocks:
            first = 0
            for i, lead in block:
                part = parts[i][...] if lead is None else parts[i][lead]
                height, width = part.shape
                whole_ref[pl.ds(first_row, height), pl.ds(first, width)] = part
                first += width
            first_row += height
        columns = branch_ref.shape[1]
        start = pl.multiple_of(place_ref[0] * columns, 128)
        branch_ref[...] = whole_ref[:, pl.ds(start, columns)]

    d_out_ref[...] = product(whole_ref[...], weight_ref[...], NT).astype(BF16)
    key, value = key_ref[...], value_ref[...]
    d_key = d_value = None
    for h in range(GROUP):
        head = pl.ds(h * HEAD_WIDTH, HEAD_WIDTH)
        for rows in pieces(query_ref.shape[0], 256):
            d_out = d_out_ref[rows, head]
            delta = jnp.sum(
                d_out.astype(F32) * out_ref[rows, head].astype(F32), axis=1, keepdims=True
            )
            probs = probs_ref[h, rows, :]
            d_scores = (probs.astype(F32) * (product(d_out, value, NT) - delta)).astype(BF16)
            d_query = turned(
                product(d_scores, key, NN) * scale, cos_ref[rows, :], -sin_ref[rows, :]
            )
            place = pl.multiple_of((g * GROUP + h) * HEAD_WIDTH, HEAD_WIDTH)
            packed_ref[rows, pl.ds(place, HEAD_WIDTH)] = d_query.astype(BF16)
            d_key_here = product(d_scores, query_ref[rows, head], TN)
            d_value_here = product(probs, d_out, TN)
            d_key = d_key_here if d_key is None else d_key + d_key_here
            d_value = d_value_here if d_value is None else d_value + d_value_here
    place = pl.multiple_of((kv_heads * GROUP + g) * HEAD_WIDTH, HEAD_WIDTH)
    packed_ref[:, pl.ds(place, HEAD_WIDTH)] = turned(
        d_key * scale, cos_ref[...], -sin_ref[...]
    ).astype(BF16)
    place = pl.multiple_of((kv_heads * (GROUP + 1) + g) * HEAD_WIDTH, HEAD_WIDTH)
    packed_ref[:, pl.ds(place, HEAD_WIDTH)] = d_value.astype(BF16)


def attend_back(queries, keys, values, probs, out, cosine, sine, parts, blocks, w_rows, columns):
    count = queries.shape[0]
    kv_heads = keys.shape[1] // HEAD_WIDTH
    wide, narrow = GROUP * HEAD_WIDTH, HEAD_WIDTH

    def column(width):
        return pl.BlockSpec((count, width), lambda g: (0, g))

    packed_shape = (count, kv_heads * (GROUP + 2) * HEAD_WIDTH)
    return pl.pallas_call(
        functools.partial(attend_back_kernel, blocks),
        out_shape=[
            jax.ShapeDtypeStruct(packed_shape, BF16),
            jax.ShapeDtypeStruct((count, columns), BF16),
        ],
        grid=(kv_heads,),
        in_specs=[
            pl.BlockSpec(memory_space=pltpu.SMEM),
            column(wide),
            column(narrow),
            column(narrow),
            pl.BlockSpec((GROUP, count, count), lambda g: (g, 0, 0)),
            column(wide),
            resident((count, HEAD_WIDTH)),
            resident((count, HEAD_WIDTH)),
            pl.BlockSpec((wide, w_rows.shape[1]), lambda g: (g, 0)),
        ]
        + [resident(p.shape) for p in parts],
        out_specs=[
            pl.BlockSpec(packed_shape, lambda g: (0, 0)),
            pl.BlockSpec((count, columns), lambda g: (0, 0)),
        ],
        scratch_shapes=[pltpu.VMEM((count, w_rows.shape[1]), BF16), pltpu.VMEM((count, wide), BF16)],
        compiler_params=kernel_params(),
        cost_estimate=cost('c_k4'),
    )(
        lax.axis_index("ctx").astype(jnp.int32)[None],
        queries,
        keys,
        values,
        probs,
        out,
        cosine,
        sine,
        w_rows,
        *parts,
    )


def square():
    return lax.axis_size("ctx") == 4


def swap(x, bit):
    return lax.ppermute(x, "ctx", [(i, i ^ bit) for i in range(4)])


def block_order():
    if square():
        return lax.axis_index("ctx") ^ jnp.arange(4, dtype=jnp.int32)
    return jnp.arange(lax.axis_size("ctx"), dtype=jnp.int32)


def gather_parts(x, *others):
    if not square():
        return [lax.all_gather(x, "ctx", axis=0, tiled=True)], [[(0, None)]]
    half = -(-x.shape[-1] // 256) * 128
    first, second = x[..., :half], x[..., half:]
    first_1 = swap(first, 1)
    second_2 = swap(second, 2)
    first_01, second_02 = jnp.stack([first, first_1]), jnp.stack([second, second_2])
    if others:
        first_01, second_02 = after(first_01, *others), after(second_02, *others)
    first_23 = swap(first_01, 2)
    second_13 = swap(second_02, 1)
    blocks = [[(0, None)], [(1, None), (4, 0)], [(3, 0), (2, None)], [(3, 1), (4, 1)]]
    return [x, first_1, second_2, first_23, second_13], blocks


def gather_ctx(x):
    if not square():
        return lax.all_gather(x, "ctx", axis=0)
    parts, blocks = gather_parts(x)
    return jnp.stack(
        [
            jnp.concatenate([parts[i] if lead is None else parts[i][lead] for i, lead in block], axis=-1)
            for block in blocks
        ]
    )


class ScatterSumCtx:
    def __init__(self, parts):
        self.parts = parts
        if square():
            self.got_first = swap(parts[0], 1)
            self.got_second = swap(parts[2], 2)

    def result(self, *others):
        if not square():
            return lax.psum_scatter(self.parts, "ctx", scatter_dimension=0, tiled=False).astype(F32)
        _, first_kept, _, second_kept = self.parts
        first = sum_low(first_kept[1], self.got_first[1])
        second = sum_low(second_kept[1], self.got_second[1])
        if others:
            first, second = after(first, *others), after(second, *others)
        last_first, last_second = swap(first, 2), swap(second, 1)
        return jnp.concatenate(
            [
                sum(t.astype(F32) for t in (first_kept[0], self.got_first[0], last_first)),
                sum(t.astype(F32) for t in (second_kept[0], self.got_second[0], last_second)),
            ],
            axis=-1,
        )


def absolute_order(blocks):
    if not square():
        return [blocks[i] for i in range(lax.axis_size("ctx"))]
    place = lax.axis_index("ctx")
    low, high = (place & 1) == 1, (place & 2) == 2
    a = [jnp.where(low, blocks[r ^ 1], blocks[r]) for r in range(4)]
    return [jnp.where(high, a[r ^ 2], a[r]) for r in range(4)]


def own_row_order(blocks):
    if not square():
        return blocks
    return [jnp.stack([blocks[s][r ^ s] for r in range(4)]) for s in range(4)]


def exchange_ctx(x):
    if not square():
        got = lax.all_to_all(x, "ctx", 0, 0, tiled=False)
        return [got[i] for i in range(lax.axis_size("ctx"))]
    order = block_order()
    parts = [lax.dynamic_index_in_dim(x, order[r], 0, keepdims=False) for r in range(4)]
    got = [parts[0]] + [swap(parts[r], r) for r in range(1, 4)]
    return absolute_order(got)


def nothing_kernel(*refs):
    del refs


def after(x, *others):
    if not square():
        return x
    return pl.pallas_call(
        nothing_kernel,
        out_shape=jax.ShapeDtypeStruct(x.shape, x.dtype),
        in_specs=anywhere((x, *others)),
        out_specs=anywhere((x,))[0],
        input_output_aliases={0: 0},
        cost_estimate=pl.CostEstimate(flops=0, bytes_accessed=0, transcendentals=0),
    )(x, *others)


def unit_halves(*weights):
    units = weights[0].shape[0]
    if not square():
        halves = [[w[: units // 2], w[units // 2 :]] for w in weights]
    else:
        place = lax.axis_index("ctx")
        blocks = [w.reshape(4, units // 4, w.shape[1]) for w in weights]

        def half(w, order):
            return jnp.concatenate(
                [lax.dynamic_index_in_dim(w, place ^ r, 0, keepdims=False) for r in order]
            )

        halves = [[half(w, (1, 3)), half(w, (2, 0))] for w in blocks]
    return jnp.concatenate([h[i] for i in range(2) for h in halves])


def lay_heads_kernel(blocks, sizes, place_ref, weight_ref, gain_ref, *refs):
    parts, (qkv_ref, out_ref, gain_attn_ref, gain_ffn_ref) = refs[:-4], refs[-4:]
    q_cols, kv_cols, out_cols, places = sizes
    head_cols = q_cols + 2 * kv_cols
    gain_attn = gain_ffn = 0.0
    for r, block in enumerate(blocks):
        place = place_ref[r]
        rows = jnp.concatenate(
            [parts[i][...] if lead is None else parts[i][lead] for i, lead in block], axis=1
        ).astype(F32)
        first = 0
        for width, start in (
            (q_cols, 0),
            (kv_cols, q_cols * places),
            (kv_cols, (q_cols + kv_cols) * places),
        ):
            columns = pl.ds(pl.multiple_of(start + place * width, 128), width)
            piece = rows[:, first : first + width]
            qkv_ref[:, columns] = piece
            gain_attn += jnp.sum(piece * weight_ref[:, columns].astype(F32), axis=1, keepdims=True)
            first += width
        columns = pl.ds(pl.multiple_of(place * out_cols, 128), out_cols)
        out_ref[:, columns] = rows[:, head_cols : head_cols + out_cols]
        gain_ffn += rows[:, head_cols + out_cols :]
    gain_ffn_ref[...] = gain_ffn.T[:1]
    gain_attn = jnp.broadcast_to(gain_attn, (gain_attn.shape[0], 128))
    gain_attn_ref[...] = gain_attn.T[:1] / gain_ref[...]


def lay_heads(parts, blocks, sizes, w_qkv, norm_attn, waits):
    rows, qkv_cols = w_qkv.shape
    q_cols, kv_cols, out_cols, places = sizes
    whole = pl.BlockSpec(memory_space=pltpu.VMEM)
    return pl.pallas_call(
        functools.partial(lay_heads_kernel, blocks, sizes),
        out_shape=[
            jax.ShapeDtypeStruct((rows, qkv_cols), F32),
            jax.ShapeDtypeStruct((rows, out_cols * places), F32),
            jax.ShapeDtypeStruct((1, rows), F32),
            jax.ShapeDtypeStruct((1, rows), F32),
        ],
        in_specs=[pl.BlockSpec(memory_space=pltpu.SMEM)]
        + [whole] * (2 + len(parts))
        + anywhere(waits),
        out_specs=[whole] * 4,
        compiler_params=kernel_params(),
        cost_estimate=cost('c_lh'),
    )(block_order(), w_qkv, norm_attn.astype(F32)[None, :], *parts, *waits)


def lay_out_kernel(place_ref, first_own, first_got, second_own, second_got, *refs):
    out_ref = refs[-1]
    step = pl.program_id(0)
    for i, block in enumerate((first_own, first_got, second_own, second_got)):

        @pl.when(step // 2 == i)
        def _(block=block):
            out_ref[...] = block[0].astype(F32)


def lay_out(first_own, first_got, second_own, second_got, waits, us):
    _, height, half = first_own.shape
    places = lax.axis_index("ctx") ^ jnp.array([0, 2, 1, 3, 0, 1, 2, 3], jnp.int32)

    def block_of(i):
        return pl.BlockSpec(
            (1, height, half), lambda g, where: (jnp.clip(g - 2 * i, 0, 1), 0, 0)
        )

    return pl.pallas_call(
        lay_out_kernel,
        out_shape=jax.ShapeDtypeStruct((4 * height, 2 * half), F32),
        grid_spec=pltpu.PrefetchScalarGridSpec(
            num_scalar_prefetch=1,
            grid=(8,),
            in_specs=[block_of(i) for i in range(4)] + anywhere(waits),
            out_specs=pl.BlockSpec((height, half), lambda g, where: (where[g], g // 4)),
        ),
        compiler_params=pltpu.CompilerParams(vmem_limit_bytes=32 * 2**20),
        cost_estimate=cost(us),
    )(places, first_own, first_got, second_own, second_got, *waits)


def sum_low(*terms):
    return sum(t.astype(F32) for t in terms).astype(BF16)


class SumCtx:
    def start_first(self, part):
        self.upper = part
        if not square():
            return
        self.got_first = swap(part[0], 1)
        self.got_third = swap(part[2], 2)

    def start_second(self, part, *others):
        self.lower = part
        if not square():
            blocks = []
            for first, upper, lower in (self.upper, part):
                second = jnp.stack([upper, lower])
                blocks.append(jnp.concatenate([first, second], axis=-1))
            whole = jnp.concatenate(blocks)
            self.whole = lax.psum(whole.reshape(-1, whole.shape[-1]), "ctx").astype(F32)
            return
        self.got_second = swap(after(part[1], *others) if others else part[1], 2)

    def arrived(self, second=False):
        if not square():
            return ()
        return (self.got_second,) if second else (self.got_first, self.got_third)

    def step_2(self, *others):
        if not square():
            return ()
        first = sum_low(self.lower[0][0], self.got_first[1])
        second = sum_low(self.upper[1], self.got_third)
        self.last_first = swap(after(first, *others) if others else first, 2)
        self.last_second = swap(after(second, *others) if others else second, 1)
        return (self.last_first, self.last_second)

    def step_3(self, *others):
        if not square():
            return ()
        self.first = sum_low(self.lower[0][1], self.got_first[0], self.last_first)
        self.second = sum_low(self.lower[2], self.got_second, self.last_second)
        if others:
            self.first = after(self.first, *others)
            self.second = after(self.second, *others)
        self.first_2 = swap(self.first, 2)
        self.second_1 = swap(self.second, 1)
        return (self.first_2, self.second_1)

    def step_4(self, *others):
        if not square():
            return ()
        self.first_02 = jnp.stack([self.first, self.first_2])
        self.second_01 = jnp.stack([self.second, self.second_1])
        if others:
            self.first_02 = after(self.first_02, *others)
            self.second_01 = after(self.second_01, *others)
        self.first_13 = swap(self.first_02, 1)
        self.second_23 = swap(self.second_01, 2)
        return (self.first_13, self.second_23)

    def result(self, waits=(), us=300):
        if not square():
            return self.whole
        return lay_out(self.first_02, self.first_13, self.second_01, self.second_23, waits, us)


def local(
    tokens,
    cotangent,
    norm_attn,
    w_qkv,
    w_out,
    norm_ffn,
    w_gate,
    w_up,
    w_down,
    seq_len,
    window,
    global_pos,
):
    places = lax.axis_size("ctx")
    place = lax.axis_index("ctx")
    shards = lax.axis_size("fsdp")
    rows = tokens.shape[1]
    width = tokens.shape[2]
    count = places * rows
    kv_heads = KEY_VALUE_HEADS // places
    q_heads = kv_heads * GROUP
    q_cols = q_heads * HEAD_WIDTH
    kv_cols = kv_heads * HEAD_WIDTH
    q_all = QUERY_HEADS * HEAD_WIDTH
    kv_all = KEY_VALUE_HEADS * HEAD_WIDTH
    out_cols = width // places
    length = seq_len[0]
    window_now = window[0]
    global_here = global_pos[0]
    x_own = tokens[0]
    cot_own = cotangent[0]

    head_cols = q_cols + 2 * kv_cols
    weights_mine = jnp.concatenate(
        [
            lax.dynamic_slice_in_dim(w_qkv, place * q_cols, q_cols, 1),
            lax.dynamic_slice_in_dim(w_qkv, q_all + place * kv_cols, kv_cols, 1),
            lax.dynamic_slice_in_dim(w_qkv, q_all + kv_all + place * kv_cols, kv_cols, 1),
            lax.dynamic_slice_in_dim(w_out, place * out_cols, out_cols, 1),
        ],
        axis=1,
    )
    weights = lax.all_gather(weights_mine, "fsdp", axis=0, tiled=True)
    gains = lax.all_gather(jnp.stack([norm_attn, norm_ffn]), "fsdp", axis=1, tiled=True)
    gain_attn = gains[0].astype(F32)
    gain_ffn = gains[1].astype(F32)
    x_parts, x_blocks = gather_parts(x_own, gains)
    cot_all = lax.all_gather(after(cot_own, *x_parts[-2:]), "fsdp", axis=0, tiled=True)
    gate_up = unit_halves(w_gate, w_up)
    down = unit_halves(w_down)
    w_rows = jnp.concatenate(
        exchange_ctx(weights[:, head_cols:].reshape(places, q_cols, out_cols)), axis=1
    )

    normed_low, packed = norm_project(x_parts, x_blocks, gain_attn[None, :], weights, head_cols)
    order = block_order()
    positions = (order[:, None] * rows + jnp.arange(rows, dtype=jnp.int32)[None, :]).reshape(count)
    cosine, sine = rope_tables(positions)
    is_global = jnp.any(positions[:, None] == global_here[None, :], axis=1)
    allowed = (
        (positions[None, :] <= positions[:, None])
        & (positions[None, :] < length)
        & (
            (positions[:, None] - positions[None, :] < window_now)
            | is_global[:, None]
            | is_global[None, :]
        )
    )
    bias = jnp.where(allowed, 0.0, NEGATIVE_FILLER)
    queries, keys, values, probs, attended_low = attend(packed, cosine, sine, bias, kv_heads)
    branch = ScatterSumCtx(product_in_parts(attended_low, w_rows, NN, width)).result()

    x_full = x_own.astype(F32)
    middle = x_full + branch
    inv_ffn = lax.rsqrt(jnp.mean(middle * middle, axis=-1, keepdims=True) + NORM_EPS)
    normed_ffn = middle * inv_ffn
    ffn_low = (normed_ffn * gain_ffn[None, :]).astype(BF16)
    ffn_all = lax.all_gather(after(ffn_low, cot_all), "fsdp", axis=0, tiled=True)
    attended_all = jnp.concatenate(
        absolute_order(own_row_order(gather_ctx(attended_low.reshape(places, rows, q_cols)))), axis=-1
    ).reshape(count, q_all)
    sum_down, sum_gate, sum_up = SumCtx(), SumCtx(), SumCtx()
    hidden, d_both, *first_t = hidden_grads(ffn_all, cot_all, gate_up, down, 0, (), (attended_all,))
    down_a = weight_grad(first_t[0], cot_all, (), "c_da")
    sum_down.start_first(down_a)
    hidden, d_both, *second_t = hidden_grads(
        ffn_all, cot_all, gate_up, down, 1, (hidden, d_both), down_a
    )
    last = (second_t[0],)
    if PLAN["o_ga"] == 0:
        gate_a = weight_grad(
            first_t[1], ffn_all, (*last, *on("w_ga_d1", sum_down.arrived())), "c_ga"
        )
        sum_gate.start_first(gate_a)
        last = gate_a
    if PLAN["o_db"]:
        down_b = weight_grad(
            second_t[0], cot_all, (*last, *on("w_db_d1", sum_down.arrived())), "c_db"
        )
        last = down_b
    d_ffn_part = rows_product(
        d_both,
        gate_up,
        (
            *last,
            *on("w_df_d1", sum_down.arrived()),
            *(on("w_df_g1", sum_gate.arrived()) if PLAN["o_ga"] == 0 else ()),
        ),
        "c_df",
    )
    d_ffn = lax.psum_scatter(d_ffn_part, "fsdp", scatter_dimension=0, tiled=True)
    last = (d_ffn_part,)
    if PLAN["o_ga"] == 1:
        gate_a = weight_grad(
            first_t[1], ffn_all, (*last, *on("w_ga_d1", sum_down.arrived())), "c_ga"
        )
        sum_gate.start_first(gate_a)
        last = gate_a
    if not PLAN["o_db"]:
        down_b = weight_grad(
            second_t[0], cot_all, (*last, *(on("w_db_g1", sum_gate.arrived()) if PLAN["o_ga"] < 2 else ())), "c_db"
        )
        last = down_b
    sum_down.start_second(down_b)
    down_2 = sum_down.step_2()
    if PLAN["o_ga"] == 2:
        gate_a = weight_grad(
            first_t[1], ffn_all, (*last, *on("w_ga_d1", sum_down.arrived())), "c_ga"
        )
        sum_gate.start_first(gate_a)
        last = gate_a
    up_a = weight_grad(first_t[2], ffn_all, (*last, *on("w_ua_g1", sum_gate.arrived())), "c_ua")
    sum_up.start_first(up_a)
    waits = (
        *up_a,
        *on("w_ou_d2", (*down_2, *sum_down.arrived(True))),
        *on("w_ou_g1", sum_gate.arrived()),
    )
    if PLAN["o_c4"]:
        ffn_part = sum_cores(*core_product(hidden, down, waits, "c_ou"))
    else:
        ffn_part = rows_product(hidden, down, waits, "c_ou")
    gate_b = weight_grad(
        second_t[1],
        ffn_all,
        (
            ffn_part,
            *on("w_gb_u1", sum_up.arrived()),
            *on("w_gb_d2", (*down_2, *sum_down.arrived(True))),
        ),
        "c_gb",
    )
    sum_gate.start_second(gate_b)
    gate_2 = sum_gate.step_2()
    down_3 = sum_down.step_3()
    up_b = weight_grad(
        second_t[2], ffn_all, (*gate_b, *on("w_ub_u1", sum_up.arrived())), "c_ub"
    )
    if not PLAN["o_r2u"]:
        sum_up.start_second(up_b)
    d_ffn = after(
        d_ffn,
        *up_b,
        *on("w_nb_d3", down_3),
        *on("w_nb_g2", gate_2),
        *on("w_nb_u1", sum_up.arrived()),
    )
    if PLAN["o_c4"]:
        ffn_sum = scatter_chips(ffn_part)
    else:
        ffn_sum = lax.psum_scatter(ffn_part, "fsdp", scatter_dimension=0, tiled=True)
    layer_out = middle + ffn_sum.astype(F32)

    d_ffn = d_ffn.astype(F32)
    scaled = d_ffn * gain_ffn[None, :]
    d_gain_ffn = jnp.sum(d_ffn * normed_ffn, axis=0)
    d_middle = cot_own.astype(F32) + inv_ffn * (
        scaled - normed_ffn * jnp.mean(scaled * normed_ffn, axis=-1, keepdims=True)
    )
    d_branch_own = d_middle.astype(BF16)
    branch_parts, branch_blocks = gather_parts(
        d_branch_own, *on("w_ag_d3", down_3), *on("w_ag_g2", gate_2)
    )
    arrived = branch_parts[-2:]
    if PLAN["o_r2u"]:
        sum_up.start_second(up_b, *arrived)
    up_2 = sum_up.step_2(*on("o_u2", arrived))
    gate_3 = sum_gate.step_3(*on("o_g3", arrived))
    down_4 = sum_down.step_4(*on("o_d4", arrived))
    d_packed, branch_cols = attend_back(
        queries,
        keys,
        values,
        probs,
        attended_low,
        cosine,
        sine,
        branch_parts,
        branch_blocks,
        w_rows,
        out_cols,
    )
    up_3 = sum_up.step_3(*on("o_u3", (d_packed,)))
    gain_cols = jnp.broadcast_to(d_gain_ffn[:, None], (width, 128))
    terms = [(normed_low, d_packed), (attended_all, branch_cols)]
    if PLAN["o_c8"]:
        by_core = rows_grad(terms, gain_cols)
        d_weights = sum_cores(*by_core)
    else:
        by_core = [plain_grad(terms, gain_cols)]
        d_weights = by_core[0]
    d_weights = after(d_weights, ffn_sum)
    d_attn_parts = product_in_parts(
        after(
            d_packed,
            d_weights if PLAN["o_dx"] else by_core[0],
            *on("w_dx_u2", up_2),
            *on("w_dx_g3", gate_3),
            *on("w_dx_d4", down_4),
        ),
        weights,
        NT,
        width,
    )
    if PLAN["o_c8"]:
        scattered = scatter_chips(d_weights)
    else:
        scattered = lax.psum_scatter(d_weights, "fsdp", scatter_dimension=0, tiled=True)
    d_attn_sum = ScatterSumCtx(d_attn_parts)
    gate_4 = sum_gate.step_4(*on("o_g4", (d_weights,)))
    up_4 = sum_up.step_4(*on("o_u4", (d_weights,)))
    grad_down = sum_down.result(d_attn_parts, "c_ld")
    parts, blocks = gather_parts(
        after(scattered, grad_down, *on("w_aw_g4", gate_4), *on("w_aw_u4", up_4))
    )
    if not square():
        rows_here = scattered.shape[0]
        parts = [parts[0].reshape(places, rows_here, -1)]
        blocks = [[(0, i)] for i in range(places)]
    d_attn = d_attn_sum.result(*on("o_dx2", parts[1:3]))
    inv_own = lax.rsqrt(jnp.mean(x_full * x_full, axis=-1, keepdims=True) + NORM_EPS)
    normed_attn = x_full * inv_own
    scaled_attn = d_attn * gain_attn[None, :]
    d_tokens = d_middle + inv_own * (
        scaled_attn - normed_attn * jnp.mean(scaled_attn * normed_attn, axis=-1, keepdims=True)
    )
    grad_gate = sum_gate.result(on("o_lg", parts[1:3]), "c_lg")
    grad_up = sum_up.result(on("o_lu", parts[1:3]), "c_lu")
    grad_qkv, grad_out, grad_gain_attn, grad_gain_ffn = lay_heads(
        parts,
        blocks,
        (q_cols, kv_cols, out_cols, places),
        w_qkv,
        norm_attn,
        on("w_lh", (grad_up,)),
    )
    return (
        layer_out.astype(BF16)[None],
        d_tokens[None],
        grad_gain_attn[0],
        grad_qkv,
        grad_out,
        grad_gain_ffn[0],
        grad_gate,
        grad_up,
        grad_down,
    )


def solution(mesh):
    return jax.shard_map(
        local,
        mesh=mesh,
        in_specs=(
            P("fsdp", "ctx", None),
            P("fsdp", "ctx", None),
            P("fsdp"),
            P("fsdp", None),
            P("fsdp", None),
            P("fsdp"),
            P("fsdp", None),
            P("fsdp", None),
            P("fsdp", None),
            P("fsdp"),
            P("fsdp"),
            P("fsdp", None),
        ),
        out_specs=(
            P("fsdp", "ctx", None),
            P("fsdp", "ctx", None),
            P("fsdp"),
            P("fsdp", None),
            P("fsdp", None),
            P("fsdp"),
            P("fsdp", None),
            P("fsdp", None),
            P("fsdp", None),
        ),
        check_vma=False,
    )
```
